32 devices in a mesh: node: 16 (over z, x, core), tp: 2 (over y).
Axes of the slice: x: 2, y: 2, z: 4, core: 2. Of those that a mesh axis runs over, the one named last changes fastest.
Arguments:
- query_rows: bfloat16 [4096, 8192], P('node', 'tp'), may hold values from -6 to 6
- key_rows: bfloat16 [4096, 1024], P('node', 'tp'), may hold values from -5 to 5
- value_rows: bfloat16 [4096, 1024], P('node', 'tp'), may hold values from -6 to 6
- out_weight: bfloat16 [8192, 4096], P('tp'), may hold values from -0.0625 to 0.0625
- out_grad: bfloat16 [4096, 4096], P(('node', 'tp')), may hold values from -6 to 6
- owner_slot: int32 [16], replicated, may hold values from 0 to 15, each once
Outputs:
- projected: bfloat16 [4096, 4096], P(('node', 'tp'))
- query_grad: bfloat16 [4096, 8192], P('node', 'tp')
- key_grad: bfloat16 [4096, 1024], P('node', 'tp')
- value_grad: bfloat16 [4096, 1024], P('node', 'tp')
The draws below stay inside these ranges and needn't reach their ends.
Inputs may be any that keep to these rules, and one draw needn't show every extreme that they name: `owner_slot`: every slot holds exactly one tree node.
All inputs are finite; a program needn't handle non-finite values.
Results may differ from the reference program's by a relative error of at most 0.017.
Values may be sent and summed in bfloat16 or wider, within the bound.
No kernel may reach another device: no remote copies, remote signals or barrier semaphores. Data moves between devices by JAX's collectives and lax.ppermute only.
A program may use at most 256 MiB of HBM per device.

```python
import jax
import jax.numpy as jnp
from jax import lax

Q_HEADS = 64
KV_HEADS = 8
HEAD_DIM = 128
D_OUT = 4096
NODE_LEN = 256
CHAIN = 8
LEAVES = 8
NODES = 16
TOKENS = 4096


def paired_draw(key):
    base = jax.random.fold_in(key, 4217)
    query_key, key_key = jax.random.split(base, 2)
    head_group = Q_HEADS // KV_HEADS
    keys_drawn = jnp.clip(jax.random.normal(key_key, (NODES, NODE_LEN, KV_HEADS, HEAD_DIM), jnp.float32), -4.5, 4.5)
    queries_drawn = jnp.clip(jax.random.normal(query_key, (NODES, NODE_LEN, KV_HEADS, head_group, HEAD_DIM), jnp.float32), -4.5, 4.5)
    return (queries_drawn.reshape(TOKENS, Q_HEADS * HEAD_DIM), keys_drawn.reshape(TOKENS, KV_HEADS * HEAD_DIM))


def draw_query_rows(key, part):
    return paired_draw(key)[0].astype(jnp.bfloat16)


def draw_key_rows(key, part):
    return paired_draw(key)[1].astype(jnp.bfloat16)


def shard_levels(rng, dims, cuts, smallest, largest):
    def one(dim, blocks):
        steps = jax.random.uniform(jax.random.fold_in(jax.random.fold_in(rng, 6), dim), (blocks,), jnp.float32, smallest / len(cuts), largest / len(cuts))
        return jnp.repeat(jnp.exp(steps), dims[dim] // blocks).reshape((-1,) + (1,) * (len(dims) - dim - 1))

    level = one(*cuts[0])
    for cut in cuts[1:]:
        level = level * one(*cut)
    return level


def bell_draw(stream_key, shape, deviation, most, cuts=(), held_as=jnp.bfloat16):
    gain = shard_levels(stream_key, shape, cuts, -0.22, 0.18) if cuts else 1.0
    values = jax.random.normal(stream_key, shape, jnp.float32) * deviation * gain
    return jnp.minimum(jnp.maximum(values, -most), most).astype(held_as)


def setup_inputs(seed: int = 0) -> dict:
    streams_of = jax.random.split(jax.random.key(seed), 7)
    query_rows = draw_query_rows(jax.random.fold_in(streams_of[6], 71), 0)
    key_rows = draw_key_rows(jax.random.fold_in(streams_of[6], 71), 0)
    value_rows = bell_draw(streams_of[2], (TOKENS, KV_HEADS * HEAD_DIM), 1.0, 6.0, ((0, 16), (1, 2)))
    out_weight = bell_draw(streams_of[3], (Q_HEADS * HEAD_DIM, D_OUT), (Q_HEADS * HEAD_DIM) ** -0.5, 0.0625, ((0, 2),))
    out_grad = bell_draw(streams_of[4], (TOKENS, D_OUT), 1.0, 6.0, ((0, 32),))
    owner_slot = jax.random.permutation(streams_of[5], NODES).astype(jnp.int32)
    return {"query_rows": query_rows, "key_rows": key_rows, "value_rows": value_rows, "out_weight": out_weight, "out_grad": out_grad, "owner_slot": owner_slot}


masked_score = -1.0e30


def tree_tables(owner_slot):
    node_count = owner_slot.shape[0]
    tree_nodes = CHAIN + LEAVES
    numbers = jnp.arange(node_count, dtype=jnp.int32)
    matches = (owner_slot[:, None] == numbers[None, :]).astype(jnp.int32)
    node_of_slot = jnp.sum(matches * numbers[:, None], axis=0).astype(jnp.int32)
    node_depth = jnp.minimum(node_of_slot % tree_nodes, CHAIN).astype(jnp.int32)
    chain_nodes = (node_of_slot // tree_nodes)[:, None] * tree_nodes + jnp.arange(CHAIN, dtype=jnp.int32)[None, :]
    ancestor_slot = owner_slot[chain_nodes].astype(jnp.int32)
    return node_depth, ancestor_slot


def reference(query_rows, key_rows, value_rows, out_weight, out_grad, owner_slot):
    node_count = owner_slot.shape[0]
    head_group = Q_HEADS // KV_HEADS
    score_scale = HEAD_DIM ** -0.5
    node_depth, ancestor_slot = tree_tables(owner_slot)
    query_blocks = query_rows.reshape(node_count, NODE_LEN, KV_HEADS, head_group, HEAD_DIM)
    key_blocks = key_rows.reshape(node_count, NODE_LEN, KV_HEADS, HEAD_DIM)
    value_blocks = value_rows.reshape(node_count, NODE_LEN, KV_HEADS, HEAD_DIM)
    upstream_all = jnp.dot(out_grad, out_weight.T, preferred_element_type=jnp.float32).astype(jnp.bfloat16)
    upstream_blocks = upstream_all.reshape(node_count, NODE_LEN, KV_HEADS, head_group, HEAD_DIM)
    positions = jnp.arange(NODE_LEN, dtype=jnp.int32)
    causal = positions[None, :] <= positions[:, None]
    levels = jnp.arange(CHAIN, dtype=jnp.int32)

    def one_slot(totals, slot_no):
        key_total, value_total = totals
        chosen = jnp.concatenate([ancestor_slot[slot_no], slot_no[None]]).astype(jnp.int32)
        keys_here = key_blocks[chosen].reshape((CHAIN + 1) * NODE_LEN, KV_HEADS, HEAD_DIM).astype(jnp.float32)
        values_here = value_blocks[chosen].reshape((CHAIN + 1) * NODE_LEN, KV_HEADS, HEAD_DIM).astype(jnp.float32)
        far_mask = jnp.repeat(levels < node_depth[slot_no], NODE_LEN)
        far_mask = jnp.broadcast_to(far_mask[None, :], (NODE_LEN, CHAIN * NODE_LEN))
        allowed = jnp.concatenate([far_mask, causal], axis=1)
        queries = query_blocks[slot_no].astype(jnp.float32)
        upstream = upstream_blocks[slot_no].astype(jnp.float32)
        scores = jnp.einsum("rkgd,skd->kgrs", queries, keys_here) * score_scale
        scores = jnp.where(allowed[None, None], scores, masked_score)
        row_max = jnp.max(scores, axis=-1, keepdims=True)
        exponent = jnp.exp(scores - row_max)
        row_sum = jnp.sum(exponent, axis=-1, keepdims=True)
        probability = exponent / row_sum
        weights = lax.optimization_barrier(probability.astype(jnp.bfloat16)).astype(jnp.float32)
        attended = jnp.einsum("kgrs,skd->rkgd", weights, values_here).astype(jnp.bfloat16)
        correction = jnp.transpose(jnp.sum(upstream * attended.astype(jnp.float32), axis=-1), (1, 2, 0))
        d_prob = jnp.einsum("rkgd,skd->kgrs", upstream, values_here)
        d_score = (probability * (d_prob - correction[..., None]) * score_scale).astype(jnp.bfloat16)
        d_score = lax.optimization_barrier(d_score).astype(jnp.float32)
        query_part = jnp.einsum("kgrs,skd->rkgd", d_score, keys_here).astype(jnp.bfloat16)
        key_part = jnp.einsum("kgrs,rkgd->skd", d_score, queries).reshape(CHAIN + 1, NODE_LEN, KV_HEADS, HEAD_DIM)
        value_part = jnp.einsum("kgrs,rkgd->skd", weights, upstream).reshape(CHAIN + 1, NODE_LEN, KV_HEADS, HEAD_DIM)
        key_total = key_total.at[chosen].add(key_part)
        value_total = value_total.at[chosen].add(value_part)
        return (key_total, value_total), (attended, query_part)

    empty_grad = jnp.zeros((node_count, NODE_LEN, KV_HEADS, HEAD_DIM), jnp.float32)
    (key_total, value_total), (attended_all, query_all) = lax.scan(
        one_slot, (empty_grad, empty_grad), jnp.arange(node_count, dtype=jnp.int32))
    attended_rows = attended_all.reshape(TOKENS, Q_HEADS * HEAD_DIM)
    projected = jnp.dot(attended_rows, out_weight, preferred_element_type=jnp.float32).astype(jnp.bfloat16)
    query_grad = query_all.reshape(TOKENS, Q_HEADS * HEAD_DIM)
    key_grad = key_total.reshape(TOKENS, KV_HEADS * HEAD_DIM).astype(jnp.bfloat16)
    value_grad = value_total.reshape(TOKENS, KV_HEADS * HEAD_DIM).astype(jnp.bfloat16)
    return (projected, query_grad, key_grad, value_grad)
```

```python
import functools

import jax
import jax.numpy as jnp
from jax import lax
from jax.experimental import pallas as pl
from jax.experimental.pallas import tpu as pltpu
from jax.sharding import PartitionSpec as P

HEAD_DIM = 128
NODE_LEN = 256
CHAIN = 8
LEAVES = 8
GROUP = 4

masked_score = -1e30
score_scale = HEAD_DIM ** (-0.5)
log2_e = 1.4426950408889634


def dot(a, b):
    return jnp.dot(a, b, preferred_element_type=jnp.float32)


def dot_nt(a, b):
    return lax.dot_general(a, b, (((1,), (1,)), ((), ())), preferred_element_type=jnp.float32)


def attend(
    lineage, depth_ref, q_ref, up_ref, far_ref, own_ref,
    att_ref, dq_ref, far_grad, own_grad,
    s_ref, p_ref, qs, ups, q_t, up_t, m_ref, l_ref, acc_ref, corr_ref, grad_t,
):
    step = pl.program_id(0)
    depth = depth_ref[0]
    heads = q_ref.shape[1] // HEAD_DIM
    rows = heads * NODE_LEN
    half = HEAD_DIM
    factor = score_scale * log2_e

    def head_rows(h):
        return pl.ds(h * NODE_LEN, NODE_LEN)

    def head_columns(h):
        return pl.ds(h * HEAD_DIM, HEAD_DIM)

    for h in range(heads):
        qs[head_rows(h), :] = q_ref[:, head_columns(h)]
        ups[head_rows(h), :] = up_ref[:, head_columns(h)]

    def fold_max(s):
        return jnp.maximum(s[:, :half], s[:, half:])

    s = dot_nt(qs[...], own_ref[:, :half])
    row = lax.broadcasted_iota(jnp.int32, (rows, NODE_LEN), 0) % NODE_LEN
    col = lax.broadcasted_iota(jnp.int32, (rows, NODE_LEN), 1)
    s = jnp.where(col <= row, s, masked_score)
    s_ref[CHAIN] = s
    m_ref[...] = fold_max(s)

    def score_block(b, carry):
        s = dot_nt(qs[...], far_ref[lineage[b], :, :half])
        s_ref[b] = s
        m_ref[...] = jnp.maximum(m_ref[...], fold_max(s))
        return carry

    lax.fori_loop(0, depth, score_block, 0)
    m_ref[...] = jnp.broadcast_to(jnp.max(m_ref[...], axis=1, keepdims=True), (rows, half))

    def weigh(b, values):
        top = m_ref[...]
        s = s_ref[b]
        p_low = jnp.exp2((s[:, :half] - top) * factor)
        p_high = jnp.exp2((s[:, half:] - top) * factor)
        p = jnp.concatenate([p_low, p_high], axis=1).astype(jnp.bfloat16)
        p_ref[b] = p
        return p_low + p_high, dot(p, values)

    part_sum, part = weigh(CHAIN, own_ref[:, half:])
    l_ref[...] = part_sum
    acc_ref[...] = part

    def forward_block(b, carry):
        part_sum, part = weigh(b, far_ref[lineage[b], :, half:])
        l_ref[...] += part_sum
        acc_ref[...] += part
        return carry

    lax.fori_loop(0, depth, forward_block, 0)
    inverse = 1.0 / jnp.broadcast_to(jnp.sum(l_ref[...], axis=1, keepdims=True), (rows, half))
    l_ref[...] = inverse
    attended = (acc_ref[...] * inverse).astype(jnp.bfloat16)
    upstream = ups[...].astype(jnp.float32)
    corr_ref[...] = jnp.broadcast_to(
        jnp.sum(upstream * attended.astype(jnp.float32), axis=1, keepdims=True), (rows, half)
    )
    for h in range(heads):
        att_ref[:, head_columns(h)] = attended[h * NODE_LEN : (h + 1) * NODE_LEN, :]
    q_scaled = qs[...].astype(jnp.float32) * (inverse * score_scale)
    q_t[...] = q_scaled.T.astype(jnp.bfloat16)
    up_t[...] = (upstream * inverse).T.astype(jnp.bfloat16)

    @pl.when(step == 0)
    def _():
        grad_t[...] = jnp.zeros_like(grad_t)

    def backward(b, keys, values):
        corr = corr_ref[...]
        p = p_ref[b]
        d_prob = dot_nt(ups[...], values)
        centred = jnp.concatenate([d_prob[:, :half] - corr, d_prob[:, half:] - corr], axis=1)
        d_score = (p.astype(jnp.float32) * centred).astype(jnp.bfloat16)
        grad_t[b, :half, :] += dot(q_t[...], d_score)
        grad_t[b, half:, :] += dot(up_t[...], p)
        return dot(d_score, keys)

    acc_ref[...] = backward(CHAIN, own_ref[:, :half], own_ref[:, half:])

    def backward_block(b, carry):
        slot = lineage[b]
        acc_ref[...] += backward(b, far_ref[slot, :, :half], far_ref[slot, :, half:])
        return carry

    lax.fori_loop(0, depth, backward_block, 0)
    query_grad = (acc_ref[...] * (l_ref[...] * score_scale)).astype(jnp.bfloat16)
    for h in range(heads):
        dq_ref[:, head_columns(h)] = query_grad[h * NODE_LEN : (h + 1) * NODE_LEN, :]

    @pl.when(step == pl.num_programs(0) - 1)
    def _():
        far_grad[...] = jnp.zeros_like(far_grad)
        own_grad[...] = grad_t[CHAIN].T

        def emit(b, carry):
            far_grad[lineage[b]] = grad_t[b].T.astype(jnp.bfloat16)
            return carry

        lax.fori_loop(0, depth, emit, 0)


def attention(kv_head, head_group, lineage, depth, query_rows, upstream, far, own):
    group = min(GROUP, head_group)
    steps = head_group // group
    slots = far.shape[0]
    width = group * HEAD_DIM
    rows = group * NODE_LEN
    first = kv_head * steps

    def heads_in(j, *_):
        return (0, first + j)

    def heads_out(j, *_):
        return (0, j)

    def whole2(j, *_):
        return (0, 0)

    def whole3(j, *_):
        return (0, 0, 0)

    pair = 2 * HEAD_DIM
    blocks = (CHAIN + 1) * head_group
    out_rows = jax.ShapeDtypeStruct((NODE_LEN, head_group * HEAD_DIM), jnp.bfloat16)
    return pl.pallas_call(
        attend,
        grid_spec=pltpu.PrefetchScalarGridSpec(
            num_scalar_prefetch=2,
            grid=(steps,),
            in_specs=[
                pl.BlockSpec((NODE_LEN, width), heads_in),
                pl.BlockSpec((NODE_LEN, width), heads_in),
                pl.BlockSpec((slots, NODE_LEN, pair), whole3),
                pl.BlockSpec((NODE_LEN, pair), whole2),
            ],
            out_specs=[
                pl.BlockSpec((NODE_LEN, width), heads_out),
                pl.BlockSpec((NODE_LEN, width), heads_out),
                pl.BlockSpec((slots, NODE_LEN, pair), whole3),
                pl.BlockSpec((NODE_LEN, pair), whole2),
            ],
            scratch_shapes=[
                pltpu.VMEM((CHAIN + 1, rows, NODE_LEN), jnp.float32),
                pltpu.VMEM((CHAIN + 1, rows, NODE_LEN), jnp.bfloat16),
                pltpu.VMEM((rows, HEAD_DIM), jnp.bfloat16),
                pltpu.VMEM((rows, HEAD_DIM), jnp.bfloat16),
                pltpu.VMEM((HEAD_DIM, rows), jnp.bfloat16),
                pltpu.VMEM((HEAD_DIM, rows), jnp.bfloat16),
                pltpu.VMEM((rows, HEAD_DIM), jnp.float32),
                pltpu.VMEM((rows, HEAD_DIM), jnp.float32),
                pltpu.VMEM((rows, HEAD_DIM), jnp.float32),
                pltpu.VMEM((rows, HEAD_DIM), jnp.float32),
                pltpu.VMEM((CHAIN + 1, pair, NODE_LEN), jnp.float32),
            ],
        ),
        out_shape=[
            out_rows,
            out_rows,
            jax.ShapeDtypeStruct((slots, NODE_LEN, pair), jnp.bfloat16),
            jax.ShapeDtypeStruct((NODE_LEN, pair), jnp.float32),
        ],
        compiler_params=pltpu.CompilerParams(
            dimension_semantics=("arbitrary",), vmem_limit_bytes=48 * 1024 * 1024
        ),
        cost_estimate=pl.CostEstimate(
            flops=12 * blocks * NODE_LEN * NODE_LEN * HEAD_DIM,
            bytes_accessed=16 * 1024 * 1024,
            transcendentals=blocks * NODE_LEN * NODE_LEN,
        ),
    )(lineage, depth, query_rows, upstream, far, own)


def exchange_sum(part, tp):
    rows = part.shape[0] // tp
    if tp != 2:
        return lax.psum_scatter(part, "tp", scatter_dimension=0, tiled=True)
    me = lax.axis_index("tp")
    away = lax.dynamic_slice_in_dim(part, (1 - me) * rows, rows, 0)
    here = lax.dynamic_slice_in_dim(part, me * rows, rows, 0)
    came = lax.ppermute(away, "tp", [(0, 1), (1, 0)])
    return (here.astype(jnp.float32) + came.astype(jnp.float32)).astype(jnp.bfloat16)


def gather_rows(block, tp):
    if tp != 2:
        return lax.all_gather(block, "tp", axis=0, tiled=True)
    me = lax.axis_index("tp")
    came = lax.ppermute(block, "tp", [(0, 1), (1, 0)])
    return jnp.where(
        me == 0, jnp.concatenate([block, came], axis=0), jnp.concatenate([came, block], axis=0)
    )


def local(tp, query_rows, key_rows, value_rows, out_weight, out_grad, owner_slot):
    node_count = owner_slot.shape[0]
    tree_nodes = CHAIN + LEAVES
    kv_width = key_rows.shape[1]
    kv_heads = kv_width // HEAD_DIM
    head_group = query_rows.shape[1] // kv_width
    my_slot = lax.axis_index("node")
    numbers = jnp.arange(node_count, dtype=jnp.int32)
    tree_node = jnp.sum(jnp.where(owner_slot == my_slot, numbers, 0))
    depth = jnp.minimum(tree_node % tree_nodes, CHAIN).reshape(1)
    lineage = lax.dynamic_slice_in_dim(owner_slot, tree_node // tree_nodes * tree_nodes, CHAIN)

    out_grad_rows = gather_rows(out_grad, tp)
    own, far = [], []
    for k in range(kv_heads):
        columns = slice(k * HEAD_DIM, (k + 1) * HEAD_DIM)
        own.append(jnp.concatenate([key_rows[:, columns], value_rows[:, columns]], axis=1))
        far.append(lax.all_gather(own[k], "node", axis=0, tiled=False))
    upstream = dot_nt(out_grad_rows, out_weight).astype(jnp.bfloat16)

    attended, query_grad, key_grad, value_grad = [], [], [], []
    for k in range(kv_heads):
        att, dq, far_part, own_part = attention(
            k, head_group, lineage, depth, query_rows, upstream, far[k], own[k]
        )
        attended.append(att)
        query_grad.append(dq)
        came = lax.psum_scatter(far_part, "node", scatter_dimension=0, tiled=False)
        total = (own_part + came.astype(jnp.float32)).astype(jnp.bfloat16)
        key_grad.append(total[:, :HEAD_DIM])
        value_grad.append(total[:, HEAD_DIM:])

    projected = exchange_sum(
        dot(jnp.concatenate(attended, axis=1), out_weight).astype(jnp.bfloat16), tp
    )
    return (
        projected,
        jnp.concatenate(query_grad, axis=1),
        jnp.concatenate(key_grad, axis=1),
        jnp.concatenate(value_grad, axis=1),
    )


def solution(mesh):
    in_specs = (
        P("node", "tp"),
        P("node", "tp"),
        P("node", "tp"),
        P("tp", None),
        P(("node", "tp"), None),
        P(),
    )
    out_specs = (P(("node", "tp"), None), P("node", "tp"), P("node", "tp"), P("node", "tp"))
    return jax.shard_map(
        functools.partial(local, mesh.shape["tp"]),
        mesh=mesh, in_specs=in_specs, out_specs=out_specs, check_vma=False,
    )
```

```python
import functools

import jax
import jax.numpy as jnp
from jax import lax
from jax.experimental import pallas as pl
from jax.experimental.pallas import tpu as pltpu
from jax.sharding import PartitionSpec as P

HEAD_DIM = 128
NODE_LEN = 256
CHAIN = 8
LEAVES = 8
GROUP = 4

masked_score = -1e30
score_scale = HEAD_DIM ** (-0.5)
log2_e = 1.4426950408889634


def dot(a, b):
    return jnp.dot(a, b, preferred_element_type=jnp.float32)


def dot_nt(a, b):
    return lax.dot_general(a, b, (((1,), (1,)), ((), ())), preferred_element_type=jnp.float32)


def attend(
    lineage, place, q_ref, up_ref, own_ref, near_0, near_1, near_2, near_3, *rest,
):
    (
    att_ref, dq_ref, keep_ref, cross_ref, away_ref, own_grad, token,
    far_ref, s_ref, p_ref, qs, ups, q_t, up_t, m_ref, l_ref, acc_ref, corr_ref, grad_t,
    ) = rest[-19:]
    step = pl.program_id(1)
    depth = place[0]
    me = place[1]
    heads = q_ref.shape[1] // HEAD_DIM
    rows = heads * NODE_LEN
    half = HEAD_DIM
    factor = score_scale * log2_e

    def head_rows(h):
        return pl.ds(h * NODE_LEN, NODE_LEN)

    def head_columns(h):
        return pl.ds(h * HEAD_DIM, HEAD_DIM)

    for h in range(heads):
        qs[head_rows(h), :] = q_ref[:, head_columns(h)]
        ups[head_rows(h), :] = up_ref[:, head_columns(h)]

    @pl.when(step == 0)
    def _():
        grad_t[...] = jnp.zeros_like(grad_t)

        def fetch(b, carry):
            away = lineage[b] ^ me
            for kind, ref in enumerate((near_0, near_1, near_2, near_3)):

                @pl.when(away % 4 == kind)
                def _():
                    far_ref[b] = ref[away // 4]

            return carry

        lax.fori_loop(0, depth, fetch, 0)

    def fold_max(s):
        return jnp.maximum(s[:, :half], s[:, half:])

    s = dot_nt(qs[...], own_ref[:, :half])
    row = lax.broadcasted_iota(jnp.int32, (rows, NODE_LEN), 0) % NODE_LEN
    col = lax.broadcasted_iota(jnp.int32, (rows, NODE_LEN), 1)
    s = jnp.where(col <= row, s, masked_score)
    s_ref[CHAIN] = s
    m_ref[...] = fold_max(s)

    def score_block(b, carry):
        s = dot_nt(qs[...], far_ref[b, :, :half])
        s_ref[b] = s
        m_ref[...] = jnp.maximum(m_ref[...], fold_max(s))
        return carry

    lax.fori_loop(0, depth, score_block, 0)
    m_ref[...] = jnp.broadcast_to(jnp.max(m_ref[...], axis=1, keepdims=True), (rows, half))

    def weigh(b, values):
        top = m_ref[...]
        s = s_ref[b]
        p_low = jnp.exp2((s[:, :half] - top) * factor)
        p_high = jnp.exp2((s[:, half:] - top) * factor)
        p = jnp.concatenate([p_low, p_high], axis=1).astype(jnp.bfloat16)
        p_ref[b] = p
        return p_low + p_high, dot(p, values)

    part_sum, part = weigh(CHAIN, own_ref[:, half:])
    l_ref[...] = part_sum
    acc_ref[...] = part

    def forward_block(b, carry):
        part_sum, part = weigh(b, far_ref[b, :, half:])
        l_ref[...] += part_sum
        acc_ref[...] += part
        return carry

    lax.fori_loop(0, depth, forward_block, 0)
    inverse = 1.0 / jnp.broadcast_to(jnp.sum(l_ref[...], axis=1, keepdims=True), (rows, half))
    l_ref[...] = inverse
    attended = (acc_ref[...] * inverse).astype(jnp.bfloat16)
    upstream = ups[...].astype(jnp.float32)
    corr_ref[...] = jnp.broadcast_to(
        jnp.sum(upstream * attended.astype(jnp.float32), axis=1, keepdims=True), (rows, half)
    )
    for h in range(heads):
        att_ref[:, head_columns(h)] = attended[h * NODE_LEN : (h + 1) * NODE_LEN, :]
    q_scaled = qs[...].astype(jnp.float32) * (inverse * score_scale)
    q_t[...] = q_scaled.T.astype(jnp.bfloat16)
    up_t[...] = (upstream * inverse).T.astype(jnp.bfloat16)

    def backward(b, keys, values):
        corr = corr_ref[...]
        p = p_ref[b]
        d_prob = dot_nt(ups[...], values)
        centred = jnp.concatenate([d_prob[:, :half] - corr, d_prob[:, half:] - corr], axis=1)
        d_score = (p.astype(jnp.float32) * centred).astype(jnp.bfloat16)
        grad_t[b, :half, :] += dot(q_t[...], d_score)
        grad_t[b, half:, :] += dot(up_t[...], p)
        return dot(d_score, keys)

    acc_ref[...] = backward(CHAIN, own_ref[:, :half], own_ref[:, half:])

    def backward_block(b, carry):
        acc_ref[...] += backward(b, far_ref[b, :, :half], far_ref[b, :, half:])
        return carry

    lax.fori_loop(0, depth, backward_block, 0)
    query_grad = (acc_ref[...] * (l_ref[...] * score_scale)).astype(jnp.bfloat16)
    for h in range(heads):
        dq_ref[:, head_columns(h)] = query_grad[h * NODE_LEN : (h + 1) * NODE_LEN, :]

    @pl.when(step == pl.num_programs(1) - 1)
    def _():
        keep_ref[...] = jnp.zeros_like(keep_ref)
        cross_ref[...] = jnp.zeros_like(cross_ref)
        away_ref[...] = jnp.zeros_like(away_ref)
        own_grad[...] = grad_t[CHAIN].T
        token[...] = jnp.zeros_like(token)

        def emit(b, carry):
            away = lineage[b] ^ me
            block = grad_t[b].T.astype(jnp.bfloat16)
            kind = away % 4
            place_z = away // 4

            @pl.when(kind == 0)
            def _():
                keep_ref[place_z, 0] = block

            @pl.when(kind == 2)
            def _():
                cross_ref[place_z, 0] = block

            @pl.when(kind % 2 == 1)
            def _():
                away_ref[kind // 2, place_z, 0] = block

            return carry

        lax.fori_loop(0, depth, emit, 0)


def attention(
    first_head, chunk_head, heads, head_group, lineage, place, query_rows, upstream, own, near, after
):
    group = min(GROUP, head_group)
    steps = head_group // group
    stride = near[0].shape[0]
    width = group * HEAD_DIM
    rows = group * NODE_LEN
    pair = 2 * HEAD_DIM

    def heads_in(i, j, *_):
        return (0, (first_head + i) * steps + j)

    def heads_out(i, j, *_):
        return (0, i * steps + j)

    def near_block(i, j, *_):
        return (0, 0, chunk_head + i)

    def own_in(i, j, *_):
        return (0, chunk_head + i)

    def own_out(i, j, *_):
        return (0, i)

    def part_block(i, j, *_):
        return (0, i, 0, 0)

    def away_block(i, j, *_):
        return (0, 0, i, 0, 0)

    blocks = (CHAIN + 1) * head_group * heads
    out_rows = jax.ShapeDtypeStruct((NODE_LEN, heads * head_group * HEAD_DIM), jnp.bfloat16)
    part = jax.ShapeDtypeStruct((stride, heads, NODE_LEN, pair), jnp.bfloat16)
    return pl.pallas_call(
        attend,
        grid_spec=pltpu.PrefetchScalarGridSpec(
            num_scalar_prefetch=2,
            grid=(heads, steps),
            in_specs=[
                pl.BlockSpec((NODE_LEN, width), heads_in),
                pl.BlockSpec((NODE_LEN, width), heads_in),
                pl.BlockSpec((NODE_LEN, pair), own_in),
            ]
            + [pl.BlockSpec((stride, NODE_LEN, pair), near_block)] * 4
            + [pl.BlockSpec(memory_space=pl.ANY)] * len(after),
            out_specs=[
                pl.BlockSpec((NODE_LEN, width), heads_out),
                pl.BlockSpec((NODE_LEN, width), heads_out),
                pl.BlockSpec((stride, 1, NODE_LEN, pair), part_block),
                pl.BlockSpec((stride, 1, NODE_LEN, pair), part_block),
                pl.BlockSpec((2, stride, 1, NODE_LEN, pair), away_block),
                pl.BlockSpec((NODE_LEN, pair), own_out),
                pl.BlockSpec((8, HEAD_DIM), lambda i, j, *_: (0, 0)),
            ],
            scratch_shapes=[
                pltpu.VMEM((CHAIN, NODE_LEN, pair), jnp.bfloat16),
                pltpu.VMEM((CHAIN + 1, rows, NODE_LEN), jnp.float32),
                pltpu.VMEM((CHAIN + 1, rows, NODE_LEN), jnp.bfloat16),
                pltpu.VMEM((rows, HEAD_DIM), jnp.bfloat16),
                pltpu.VMEM((rows, HEAD_DIM), jnp.bfloat16),
                pltpu.VMEM((HEAD_DIM, rows), jnp.bfloat16),
                pltpu.VMEM((HEAD_DIM, rows), jnp.bfloat16),
                pltpu.VMEM((rows, HEAD_DIM), jnp.float32),
                pltpu.VMEM((rows, HEAD_DIM), jnp.float32),
                pltpu.VMEM((rows, HEAD_DIM), jnp.float32),
                pltpu.VMEM((rows, HEAD_DIM), jnp.float32),
                pltpu.VMEM((CHAIN + 1, pair, NODE_LEN), jnp.float32),
            ],
        ),
        out_shape=[
            out_rows,
            out_rows,
            part,
            part,
            jax.ShapeDtypeStruct((2, stride, heads, NODE_LEN, pair), jnp.bfloat16),
            jax.ShapeDtypeStruct((NODE_LEN, heads * pair), jnp.float32),
            jax.ShapeDtypeStruct((8, HEAD_DIM), jnp.float32),
        ],
        compiler_params=pltpu.CompilerParams(
            dimension_semantics=("arbitrary", "arbitrary"), vmem_limit_bytes=60 * 1024 * 1024
        ),
        cost_estimate=pl.CostEstimate(
            flops=12 * blocks * NODE_LEN * NODE_LEN * HEAD_DIM,
            bytes_accessed=heads * 16 * 1024 * 1024,
            transcendentals=blocks * NODE_LEN * NODE_LEN,
        ),
    )(lineage, place, query_rows, upstream, own, *near, *after)


def swap(block, mask, nodes):
    return lax.ppermute(block, "node", [(i, i ^ mask) for i in range(nodes)])


def gather_near(own, nodes):
    stride = nodes // 4
    line = jnp.stack([own] + [swap(own, 4 * d, nodes) for d in range(1, stride)])
    cross = swap(line, 2, nodes)
    return line, swap(line, 1, nodes), cross, swap(cross, 1, nodes)


def scatter_sum(keep, cross, away, own_part, nodes):
    f32 = jnp.float32
    stride = nodes // 4
    came = swap(away, 1, nodes)
    zero = yield [away]
    cross = (cross.astype(f32) + (came[1].astype(f32) + zero)).astype(jnp.bfloat16)
    keep = keep.astype(f32) + (came[0].astype(f32) + zero)
    came = swap(cross, 2, nodes)
    zero = yield [cross]
    keep = keep + (came.astype(f32) + zero)
    sent = [keep[d].astype(jnp.bfloat16) for d in range(1, stride)]
    came = [swap(part, 4 * (d + 1), nodes) for d, part in enumerate(sent)]
    zero = yield sent
    total = own_part + (keep[0] + zero)
    for part in came:
        total = total + part.astype(f32)
    yield [total.astype(jnp.bfloat16)]


def exchange_sum(part, tp):
    rows = part.shape[0] // tp
    if tp != 2:
        return lax.psum_scatter(part, "tp", scatter_dimension=0, tiled=True)
    me = lax.axis_index("tp")
    away = lax.dynamic_slice_in_dim(part, (1 - me) * rows, rows, 0)
    here = lax.dynamic_slice_in_dim(part, me * rows, rows, 0)
    came = lax.ppermute(away, "tp", [(0, 1), (1, 0)])
    return (here.astype(jnp.float32) + came.astype(jnp.float32)).astype(jnp.bfloat16)


def gather_rows(block, tp):
    if tp != 2:
        return lax.all_gather(block, "tp", axis=0, tiled=True)
    me = lax.axis_index("tp")
    came = lax.ppermute(block, "tp", [(0, 1), (1, 0)])
    return jnp.where(
        me == 0, jnp.concatenate([block, came], axis=0), jnp.concatenate([came, block], axis=0)
    )


def local(tp, nodes, query_rows, key_rows, value_rows, out_weight, out_grad, owner_slot):
    node_count = owner_slot.shape[0]
    tree_nodes = CHAIN + LEAVES
    kv_width = key_rows.shape[1]
    kv_heads = kv_width // HEAD_DIM
    head_group = query_rows.shape[1] // kv_width
    pair = 2 * HEAD_DIM
    my_slot = lax.axis_index("node")
    numbers = jnp.arange(node_count, dtype=jnp.int32)
    tree_node = jnp.sum(jnp.where(owner_slot == my_slot, numbers, 0))
    depth = jnp.minimum(tree_node % tree_nodes, CHAIN)
    place = jnp.stack([depth, my_slot]).astype(jnp.int32)
    lineage = lax.dynamic_slice_in_dim(owner_slot, tree_node // tree_nodes * tree_nodes, CHAIN)

    out_grad_rows = gather_rows(out_grad, tp)
    wide = min(2, kv_heads)
    own, near = [], []
    for c in range(kv_heads // wide):
        parts = []
        for k in range(c * wide, (c + 1) * wide):
            columns = slice(k * HEAD_DIM, (k + 1) * HEAD_DIM)
            parts += [key_rows[:, columns], value_rows[:, columns]]
        own.append(jnp.concatenate(parts, axis=1))
        near.append(gather_near(own[c], nodes))
    upstream = dot_nt(out_grad_rows, out_weight).astype(jnp.bfloat16)

    calls = [(0, wide)] + [(k, 1) for k in range(wide, kv_heads)]
    attended, query_grad, sums, sent = [], [], [], []
    for first, heads in calls:
        c = first // wide
        att, dq, keep, cross, away, own_part, token = attention(
            first, first % wide, heads, head_group, lineage, place,
            query_rows, upstream, own[c], near[c], sent,
        )
        attended.append(att)
        query_grad.append(dq)
        own_part = jnp.stack([own_part[:, i * pair : (i + 1) * pair] for i in range(heads)])
        zero = token[0, 0]
        sent = [part for chain in sums for part in chain.send(zero)]
        sums.append(scatter_sum(keep, cross, away, own_part, nodes))
        sent += next(sums[-1])

    projected = dot(jnp.concatenate(attended, axis=1), out_weight).astype(jnp.bfloat16)
    projected = exchange_sum(projected, tp)
    totals = [None] * len(sums)
    left = [max(1, 3 - (len(sums) - 1 - n)) for n in range(len(sums))]
    for turn in range(3):
        for n in range(len(sums)):
            if turn < left[n]:
                totals[n] = sums[n].send(zero)[0]
    key_grad, value_grad = [], []
    for (first, heads), total in zip(calls, totals):
        for i in range(heads):
            key_grad.append(total[i, :, :HEAD_DIM])
            value_grad.append(total[i, :, HEAD_DIM:])
    return (
        projected,
        jnp.concatenate(query_grad, axis=1),
        jnp.concatenate(key_grad, axis=1),
        jnp.concatenate(value_grad, axis=1),
    )


def solution(mesh):
    in_specs = (
        P("node", "tp"),
        P("node", "tp"),
        P("node", "tp"),
        P("tp", None),
        P(("node", "tp"), None),
        P(),
    )
    out_specs = (P(("node", "tp"), None), P("node", "tp"), P("node", "tp"), P("node", "tp"))
    return jax.shard_map(
        functools.partial(local, mesh.shape["tp"], mesh.shape["node"]),
        mesh=mesh, in_specs=in_specs, out_specs=out_specs, check_vma=False,
    )
```

```python
import functools

import jax
import jax.numpy as jnp
from jax import lax
from jax.experimental import pallas as pl
from jax.experimental.pallas import tpu as pltpu
from jax.sharding import PartitionSpec as P

HEAD_DIM = 128
NODE_LEN = 256
CHAIN = 8
LEAVES = 8
GROUP = 8

masked_score = -1e30
score_scale = HEAD_DIM ** (-0.5)
log2_e = 1.4426950408889634


def dot(a, b):
    return jnp.dot(a, b, preferred_element_type=jnp.float32)


def dot_nt(a, b):
    return lax.dot_general(a, b, (((1,), (1,)), ((), ())), preferred_element_type=jnp.float32)


def attend(near_count, part_count, lineage, place, q_ref, up_ref, own_ref, *refs):
    near = refs[:near_count]
    tail = refs[len(refs) - 16 - part_count :]
    att_ref, dq_ref, own_grad, token = tail[:4]
    parts = tail[4 : 4 + part_count]
    (
        far_ref, s_ref, p_ref, qs, ups, q_t, up_t, m_ref, l_ref, acc_ref, corr_ref, grad_t,
    ) = tail[4 + part_count :]
    step = pl.program_id(1)
    depth = place[0]
    me = place[1]
    heads = q_ref.shape[1] // HEAD_DIM
    rows = heads * NODE_LEN
    half = HEAD_DIM
    factor = score_scale * log2_e

    def head_rows(h):
        return pl.ds(h * NODE_LEN, NODE_LEN)

    def head_columns(h):
        return pl.ds(h * HEAD_DIM, HEAD_DIM)

    for h in range(heads):
        qs[head_rows(h), :] = q_ref[:, head_columns(h)]
        ups[head_rows(h), :] = up_ref[:, head_columns(h)]

    @pl.when(step == 0)
    def _():
        grad_t[...] = jnp.zeros_like(grad_t)

        def fetch(b, carry):
            if near_count == 1:
                far_ref[b] = near[0][lineage[b]]
                return carry
            away = lineage[b] ^ me
            for kind in range(near_count):

                @pl.when(away % 4 == kind)
                def _():
                    far_ref[b] = near[kind][away // 4]

            return carry

        lax.fori_loop(0, depth, fetch, 0)

    def fold_max(s):
        return jnp.maximum(s[:, :half], s[:, half:])

    s = dot_nt(qs[...], own_ref[:, :half])
    row = lax.broadcasted_iota(jnp.int32, (rows, NODE_LEN), 0) % NODE_LEN
    col = lax.broadcasted_iota(jnp.int32, (rows, NODE_LEN), 1)
    s = jnp.where(col <= row, s, masked_score)
    s_ref[CHAIN] = s
    m_ref[...] = fold_max(s)

    def score_block(b, carry):
        s = dot_nt(qs[...], far_ref[b, :, :half])
        s_ref[b] = s
        m_ref[...] = jnp.maximum(m_ref[...], fold_max(s))
        return carry

    lax.fori_loop(0, depth, score_block, 0)
    m_ref[...] = jnp.broadcast_to(jnp.max(m_ref[...], axis=1, keepdims=True), (rows, half))

    def weigh(b, values):
        top = m_ref[...]
        s = s_ref[b]
        p_low = jnp.exp2((s[:, :half] - top) * factor)
        p_high = jnp.exp2((s[:, half:] - top) * factor)
        p = jnp.concatenate([p_low, p_high], axis=1).astype(jnp.bfloat16)
        p_ref[b] = p
        return p_low + p_high, dot(p, values)

    part_sum, part = weigh(CHAIN, own_ref[:, half:])
    l_ref[...] = part_sum
    acc_ref[...] = part

    def forward_block(b, carry):
        part_sum, part = weigh(b, far_ref[b, :, half:])
        l_ref[...] += part_sum
        acc_ref[...] += part
        return carry

    lax.fori_loop(0, depth, forward_block, 0)
    inverse = 1.0 / jnp.broadcast_to(jnp.sum(l_ref[...], axis=1, keepdims=True), (rows, half))
    l_ref[...] = inverse
    attended = (acc_ref[...] * inverse).astype(jnp.bfloat16)
    upstream = ups[...].astype(jnp.float32)
    corr_ref[...] = jnp.broadcast_to(
        jnp.sum(upstream * attended.astype(jnp.float32), axis=1, keepdims=True), (rows, half)
    )
    for h in range(heads):
        att_ref[:, head_columns(h)] = attended[h * NODE_LEN : (h + 1) * NODE_LEN, :]
    q_scaled = qs[...].astype(jnp.float32) * (inverse * score_scale)
    q_t[...] = q_scaled.astype(jnp.bfloat16).T
    up_t[...] = (upstream * inverse).astype(jnp.bfloat16).T

    def backward(b, keys, values):
        corr = corr_ref[...]
        p = p_ref[b]
        d_prob = dot_nt(ups[...], values)
        centred = jnp.concatenate([d_prob[:, :half] - corr, d_prob[:, half:] - corr], axis=1)
        d_score = (p.astype(jnp.float32) * centred).astype(jnp.bfloat16)
        grad_t[b, :half, :] += dot(q_t[...], d_score)
        grad_t[b, half:, :] += dot(up_t[...], p)
        return dot(d_score, keys)

    acc_ref[...] = backward(CHAIN, own_ref[:, :half], own_ref[:, half:])

    def backward_block(b, carry):
        acc_ref[...] += backward(b, far_ref[b, :, :half], far_ref[b, :, half:])
        return carry

    lax.fori_loop(0, depth, backward_block, 0)
    query_grad = (acc_ref[...] * (l_ref[...] * score_scale)).astype(jnp.bfloat16)
    for h in range(heads):
        dq_ref[:, head_columns(h)] = query_grad[h * NODE_LEN : (h + 1) * NODE_LEN, :]

    @pl.when(step == pl.num_programs(1) - 1)
    def _():
        for part in parts:
            part[...] = jnp.zeros_like(part)
        own_grad[...] = grad_t[CHAIN].T
        token[...] = jnp.zeros_like(token)

        def emit(b, carry):
            block = grad_t[b].astype(jnp.bfloat16).T
            if part_count == 1:
                parts[0][lineage[b], 0] = block
                return carry
            keep_ref, cross_ref, away_ref = parts
            away = lineage[b] ^ me
            kind = away % 4
            place_z = away // 4

            @pl.when(kind == 0)
            def _():
                keep_ref[place_z, 0] = block

            @pl.when(kind == 2)
            def _():
                cross_ref[place_z, 0] = block

            @pl.when(kind % 2 == 1)
            def _():
                away_ref[kind // 2, place_z, 0] = block

            return carry

        lax.fori_loop(0, depth, emit, 0)


def attention(
    first_head, chunk_head, heads, head_group, nodes, by_slot,
    lineage, place, query_rows, upstream, own, near, after,
):
    group = min(GROUP, head_group)
    steps = head_group // group
    stride = nodes // 4
    width = group * HEAD_DIM
    rows = group * NODE_LEN
    pair = 2 * HEAD_DIM

    def query_in(i, j, *_):
        return (0, (first_head + i) * steps + j)

    def upstream_in(i, j, *_):
        return (0, (chunk_head + i) * steps + j)

    def heads_out(i, j, *_):
        return (0, i * steps + j)

    def near_block(i, j, *_):
        return (0, 0, chunk_head + i)

    def own_in(i, j, *_):
        return (0, chunk_head + i)

    def own_out(i, j, *_):
        return (0, i)

    def part_block(i, j, *_):
        return (0, i, 0, 0)

    def away_block(i, j, *_):
        return (0, 0, i, 0, 0)

    def token_block(i, j, *_):
        return (0, 0)

    def part(count):
        return (
            pl.BlockSpec((count, 1, NODE_LEN, pair), part_block),
            jax.ShapeDtypeStruct((count, heads, NODE_LEN, pair), jnp.bfloat16),
        )

    if by_slot:
        parts = [part(nodes)]
    else:
        away = (
            pl.BlockSpec((2, stride, 1, NODE_LEN, pair), away_block),
            jax.ShapeDtypeStruct((2, stride, heads, NODE_LEN, pair), jnp.bfloat16),
        )
        parts = [part(stride), part(stride), away]
    blocks = (CHAIN + 1) * head_group * heads
    out_rows = jax.ShapeDtypeStruct((NODE_LEN, heads * head_group * HEAD_DIM), jnp.bfloat16)
    return pl.pallas_call(
        functools.partial(attend, len(near), len(parts)),
        grid_spec=pltpu.PrefetchScalarGridSpec(
            num_scalar_prefetch=2,
            grid=(heads, steps),
            in_specs=[
                pl.BlockSpec((NODE_LEN, width), query_in),
                pl.BlockSpec((NODE_LEN, width), upstream_in),
                pl.BlockSpec((NODE_LEN, pair), own_in),
            ]
            + [pl.BlockSpec((block.shape[0], NODE_LEN, pair), near_block) for block in near]
            + [pl.BlockSpec(memory_space=pl.ANY)] * len(after),
            out_specs=[
                pl.BlockSpec((NODE_LEN, width), heads_out),
                pl.BlockSpec((NODE_LEN, width), heads_out),
                pl.BlockSpec((NODE_LEN, pair), own_out),
                pl.BlockSpec((8, HEAD_DIM), token_block),
            ]
            + [spec for spec, _ in parts],
            scratch_shapes=[
                pltpu.VMEM((CHAIN, NODE_LEN, pair), jnp.bfloat16),
                pltpu.VMEM((CHAIN + 1, rows, NODE_LEN), jnp.float32),
                pltpu.VMEM((CHAIN + 1, rows, NODE_LEN), jnp.bfloat16),
                pltpu.VMEM((rows, HEAD_DIM), jnp.bfloat16),
                pltpu.VMEM((rows, HEAD_DIM), jnp.bfloat16),
                pltpu.VMEM((HEAD_DIM, rows), jnp.bfloat16),
                pltpu.VMEM((HEAD_DIM, rows), jnp.bfloat16),
                pltpu.VMEM((rows, HEAD_DIM), jnp.float32),
                pltpu.VMEM((rows, HEAD_DIM), jnp.float32),
                pltpu.VMEM((rows, HEAD_DIM), jnp.float32),
                pltpu.VMEM((rows, HEAD_DIM), jnp.float32),
                pltpu.VMEM((CHAIN + 1, pair, NODE_LEN), jnp.float32),
            ],
        ),
        out_shape=[
            out_rows,
            out_rows,
            jax.ShapeDtypeStruct((NODE_LEN, heads * pair), jnp.float32),
            jax.ShapeDtypeStruct((8, HEAD_DIM), jnp.float32),
        ]
        + [shape for _, shape in parts],
        compiler_params=pltpu.CompilerParams(
            dimension_semantics=("arbitrary", "arbitrary"), vmem_limit_bytes=60 * 1024 * 1024
        ),
        cost_estimate=pl.CostEstimate(
            flops=12 * blocks * NODE_LEN * NODE_LEN * HEAD_DIM,
            bytes_accessed=heads * 16 * 1024 * 1024,
            transcendentals=blocks * NODE_LEN * NODE_LEN,
        ),
    )(lineage, place, query_rows, upstream, own, *near, *after)


def zero_of(value):
    return jnp.minimum(jnp.abs(value.astype(jnp.float32)), 0.0)


def swap(block, mask, nodes):
    return lax.ppermute(block, "node", [(i, i ^ mask) for i in range(nodes)])


def when_there(value, parts):
    for part in parts:
        value = value + zero_of(part[(0,) * part.ndim]).astype(value.dtype)
    return value


def gather_near(own, nodes, zero):
    stride = nodes // 4
    line = jnp.stack([own] + [swap(own, 4 * d, nodes) for d in range(1, stride)])
    line = line + zero.astype(line.dtype)
    cross = swap(line, 2, nodes)
    return line, swap(line, 1, nodes), cross, swap(cross, 1, nodes)


def scatter_sum(keep, cross, away, own_part, nodes):
    f32 = jnp.float32
    stride = nodes // 4
    came = swap(away, 1, nodes)
    zero = yield [away]
    cross = (cross.astype(f32) + (came[1].astype(f32) + zero)).astype(jnp.bfloat16)
    keep = keep.astype(f32) + (came[0].astype(f32) + zero)
    came = swap(cross, 2, nodes)
    zero = yield [cross]
    keep = keep + (came.astype(f32) + zero)
    sent = [keep[d].astype(jnp.bfloat16) for d in range(1, stride)]
    came = [swap(part, 4 * (d + 1), nodes) for d, part in enumerate(sent)]
    zero = yield sent
    total = own_part + (keep[0] + zero)
    for part in came:
        total = total + part.astype(f32)
    return total.astype(jnp.bfloat16)


def other_rows(block, tp):
    if tp != 2:
        whole = lax.all_gather(block, "tp", axis=0, tiled=True)
        return whole, whole
    me = lax.axis_index("tp")
    came = lax.ppermute(block, "tp", [(0, 1), (1, 0)])
    return (
        jnp.where(
            me == 0, jnp.concatenate([block, came], axis=0), jnp.concatenate([came, block], axis=0)
        ),
        came,
    )


def local(tp, nodes, query_rows, key_rows, value_rows, out_weight, out_grad, owner_slot):
    bf16, f32 = jnp.bfloat16, jnp.float32
    node_count = owner_slot.shape[0]
    tree_nodes = CHAIN + LEAVES
    kv_width = key_rows.shape[1]
    kv_heads = kv_width // HEAD_DIM
    head_group = query_rows.shape[1] // kv_width
    pair = 2 * HEAD_DIM
    my_slot = lax.axis_index("node")
    numbers = jnp.arange(node_count, dtype=jnp.int32)
    tree_node = jnp.sum(jnp.where(owner_slot == my_slot, numbers, 0))
    depth = jnp.minimum(tree_node % tree_nodes, CHAIN)
    place = jnp.stack([depth, my_slot]).astype(jnp.int32)
    lineage = lax.dynamic_slice_in_dim(owner_slot, tree_node // tree_nodes * tree_nodes, CHAIN)

    wide = min(2, kv_heads)
    chunks = [(0, wide)] + ([(wide, kv_heads - wide)] if kv_heads > wide else [])
    calls = [(0, 0, wide)] + [(1, k, 1) for k in range(wide, kv_heads)]

    out_grad_rows, came = other_rows(out_grad, tp)
    own, near, upstream = [], [], []
    for first, heads in chunks:
        packed = []
        for k in range(first, first + heads):
            columns = slice(k * HEAD_DIM, (k + 1) * HEAD_DIM)
            packed += [key_rows[:, columns], value_rows[:, columns]]
        packed = jnp.concatenate(packed, axis=1)
        own.append(packed)
        if first == 0:
            near.append(gather_near(packed, nodes, zero_of(came[0, 0])))
        else:
            packed = packed + zero_of(near[0][0][0, 0, 0]).astype(bf16)
            near.append([lax.all_gather(packed, "node", axis=0, tiled=False)])
        width = head_group * HEAD_DIM
        weight_rows = out_weight[first * width : (first + heads) * width]
        upstream.append(dot_nt(out_grad_rows, weight_rows).astype(bf16))

    attended, query_grad, sums, sent = [], [], [], []
    first_sum = None
    for n, (c, first, heads) in enumerate(calls):
        by_slot = n == 0 and len(calls) > 1
        att, dq, own_part, token, *parts = attention(
            first, first - chunks[c][0], heads, head_group, nodes, by_slot,
            lineage, place, query_rows, upstream[c], own[c], near[c], sent,
        )
        attended.append(att)
        query_grad.append(dq)
        own_part = jnp.stack([own_part[:, i * pair : (i + 1) * pair] for i in range(heads)])
        zero = token[0, 0]
        sent = [part for chain in sums for part in chain.send(zero)]
        if by_slot:
            first_sum = (own_part, lax.psum_scatter(parts[0], "node", scatter_dimension=0, tiled=False))
            sent = [token]
        else:
            sums.append(scatter_sum(*parts, own_part, nodes))
            sent += next(sums[-1])

    attended = jnp.concatenate(attended, axis=1)
    if tp == 2:
        rows = attended.shape[0] // tp
        me = lax.axis_index("tp")
        away_rows = when_there(lax.dynamic_slice_in_dim(attended, (1 - me) * rows, rows, 0), sent)
        away = dot(away_rows, out_weight).astype(bf16)
        came = lax.ppermute(away, "tp", [(0, 1), (1, 0)])
        zero = zero_of(away[0, 0])
        sent = [part for chain in sums for part in chain.send(zero)]
        here_rows = when_there(lax.dynamic_slice_in_dim(attended, me * rows, rows, 0), sent)
        here = lax.optimization_barrier(dot(here_rows, out_weight))
        zero = zero_of(here[0, 0])
        projected = (here + came.astype(f32)).astype(bf16)
    else:
        projected = dot(attended, out_weight).astype(bf16)
        projected = lax.psum_scatter(projected, "tp", scatter_dimension=0, tiled=True)
    totals = {}
    while len(totals) < len(sums):
        for n, chain in enumerate(sums):
            if n not in totals:
                try:
                    chain.send(zero)
                except StopIteration as end:
                    totals[n] = end.value
    totals = [totals[n] for n in range(len(sums))]
    if first_sum is not None:
        own_part, came = first_sum
        zero = zero_of(totals[-1][0, 0, 0])
        totals = [(own_part + (came.astype(f32) + zero)).astype(bf16)] + totals
    key_grad = [total[i, :, :HEAD_DIM] for total in totals for i in range(total.shape[0])]
    value_grad = [total[i, :, HEAD_DIM:] for total in totals for i in range(total.shape[0])]
    return (
        projected,
        jnp.concatenate(query_grad, axis=1),
        jnp.concatenate(key_grad, axis=1),
        jnp.concatenate(value_grad, axis=1),
    )


def solution(mesh):
    in_specs = (
        P("node", "tp"),
        P("node", "tp"),
        P("node", "tp"),
        P("tp", None),
        P(("node", "tp"), None),
        P(),
    )
    out_specs = (P(("node", "tp"), None), P("node", "tp"), P("node", "tp"), P("node", "tp"))
    return jax.shard_map(
        functools.partial(local, mesh.shape["tp"], mesh.shape["node"]),
        mesh=mesh, in_specs=in_specs, out_specs=out_specs, check_vma=False,
    )
```

```python
import functools

import jax
import jax.numpy as jnp
from jax import lax
from jax.experimental import pallas as pl
from jax.experimental.pallas import tpu as pltpu
from jax.sharding import PartitionSpec as P

HEAD_DIM = 128
NODE_LEN = 256
CHAIN = 8
LEAVES = 8
PAIR = 2 * HEAD_DIM
COLUMNS = 512

masked_score = -1e30
score_scale = HEAD_DIM ** (-0.5)
log2_e = 1.4426950408889634


def dot(a, b):
    return jnp.dot(a, b, preferred_element_type=jnp.float32)


def dot_nt(a, b):
    return lax.dot_general(a, b, (((1,), (1,)), ((), ())), preferred_element_type=jnp.float32)


def attend(layout, lineage, place, *refs):
    near_count, after_count, chunk_head, by_slot, old_count, head = layout
    q_any, own_any, out_grad_any, weight_any = refs[:4]
    near = refs[4 : 4 + near_count]
    old = refs[4 + near_count : 4 + near_count + old_count]
    rest = refs[4 + near_count + old_count + after_count :]
    part_count = 1 if by_slot else 3
    dq_any, proj_any, own_any_grad = rest[:3]
    parts = rest[3 : 3 + part_count]
    (
        far_ref, own_ref, out_grad, weight, proj, att, s_ref, p_ref, qs, ups, q_t, up_t,
        m_ref, l_ref, acc_ref, own_grad, slots, far_sem, q_sem, sem,
    ) = rest[3 + part_count :]
    depth = place[0]
    me = place[1]
    rows = qs.shape[0]
    heads = rows // NODE_LEN
    half = HEAD_DIM
    width = heads * HEAD_DIM
    factor = score_scale * log2_e
    stride = slots.shape[0] // 4

    def head_rows(h):
        return pl.ds(h * NODE_LEN, NODE_LEN)

    def head_columns(h, first=0):
        return pl.ds(first + h * HEAD_DIM, HEAD_DIM)

    q_copies = [
        pltpu.make_async_copy(
            q_any.at[:, head_columns(h, head * width)], qs.at[head_rows(h), :], q_sem.at[h]
        )
        for h in range(heads)
    ]
    own_copy = pltpu.make_async_copy(
        own_any.at[:, pl.ds(chunk_head * PAIR, PAIR)], own_ref, sem.at[0]
    )
    weight_copy = pltpu.make_async_copy(
        weight_any.at[pl.ds(head * width, width), :], weight, sem.at[1]
    )
    out_grad_copy = pltpu.make_async_copy(out_grad_any, out_grad, sem.at[2])
    for copy in [own_copy] + q_copies:
        copy.start()

    def far_copy(source, index, b):
        return pltpu.make_async_copy(
            source.at[index, :, pl.ds(chunk_head * PAIR, PAIR)], far_ref.at[b], far_sem.at[b]
        )

    def fetch(b, carry):
        if near_count == 1:
            far_copy(near[0], lineage[b], b).start()
            return carry
        away = lineage[b] ^ me
        for kind in range(near_count):

            @pl.when(away % 4 == kind)
            def _():
                far_copy(near[kind], away // 4, b).start()

        return carry

    lax.fori_loop(0, depth, fetch, 0)
    weight_copy.start()
    out_grad_copy.start()
    if head > 0:
        proj_copy = pltpu.make_async_copy(old[1], proj, sem.at[3])
        proj_copy.start()

    def fold_max(s):
        return jnp.maximum(s[:, :half], s[:, half:])

    for copy in [own_copy] + q_copies:
        copy.wait()
    s = dot_nt(qs[...], own_ref[:, :half])
    row = lax.broadcasted_iota(jnp.int32, (rows, NODE_LEN), 0) % NODE_LEN
    col = lax.broadcasted_iota(jnp.int32, (rows, NODE_LEN), 1)
    s = jnp.where(col <= row, s, masked_score)
    s_ref[CHAIN] = s
    m_ref[...] = fold_max(s)

    def score_block(b, carry):
        far_copy(near[0], 0, b).wait()
        s = dot_nt(qs[...], far_ref[b, :, :half])
        s_ref[b] = s
        m_ref[...] = jnp.maximum(m_ref[...], fold_max(s))
        return carry

    lax.fori_loop(0, depth, score_block, 0)
    m_ref[...] = jnp.broadcast_to(jnp.max(m_ref[...], axis=1, keepdims=True), (rows, half))

    def weigh(b, values):
        top = m_ref[...]
        s = s_ref[b]
        p_low = jnp.exp2((s[:, :half] - top) * factor)
        p_high = jnp.exp2((s[:, half:] - top) * factor)
        p = jnp.concatenate([p_low, p_high], axis=1).astype(jnp.bfloat16)
        p_ref[b] = p
        return p_low + p_high, dot(p, values)

    part_sum, part = weigh(CHAIN, own_ref[:, half:])
    l_ref[...] = part_sum
    acc_ref[...] = part

    def forward_block(b, carry):
        part_sum, part = weigh(b, far_ref[b, :, half:])
        l_ref[...] += part_sum
        acc_ref[...] += part
        return carry

    lax.fori_loop(0, depth, forward_block, 0)
    inverse = 1.0 / jnp.broadcast_to(jnp.sum(l_ref[...], axis=1, keepdims=True), (rows, half))
    l_ref[...] = inverse
    attended = (acc_ref[...] * inverse).astype(jnp.bfloat16)
    for h in range(heads):
        att[:, head_columns(h)] = attended[h * NODE_LEN : (h + 1) * NODE_LEN, :]

    weight_copy.wait()
    out_grad_copy.wait()
    for h in range(0, heads, 2):
        count = min(2, heads - h)
        two = dot_nt(out_grad[...], weight[h * HEAD_DIM : (h + count) * HEAD_DIM, :])
        for i in range(count):
            ups[head_rows(h + i), :] = two[:, i * HEAD_DIM : (i + 1) * HEAD_DIM].astype(jnp.bfloat16)
    if head > 0:
        proj_copy.wait()

    def project(n, carry):
        columns = pl.ds(pl.multiple_of(n * COLUMNS, COLUMNS), COLUMNS)
        share = dot(att[...], weight[:, columns])
        proj[:, columns] = share if head == 0 else proj[:, columns] + share
        return carry

    lax.fori_loop(0, weight.shape[1] // COLUMNS, project, 0)
    proj_out = pltpu.make_async_copy(proj, proj_any, sem.at[4])
    proj_out.start()

    upstream = ups[...].astype(jnp.float32)
    corr_ref = m_ref
    corr_ref[...] = jnp.broadcast_to(
        jnp.sum(upstream * attended.astype(jnp.float32), axis=1, keepdims=True), (rows, half)
    )
    q_t[...] = (qs[...].astype(jnp.float32) * (inverse * score_scale)).astype(jnp.bfloat16).T
    up_t[...] = (upstream * inverse).astype(jnp.bfloat16).T

    def backward(b, keys, values):
        corr = corr_ref[...]
        p = p_ref[b]
        d_prob = dot_nt(ups[...], values)
        centred = jnp.concatenate([d_prob[:, :half] - corr, d_prob[:, half:] - corr], axis=1)
        d_score = (p.astype(jnp.float32) * centred).astype(jnp.bfloat16)
        grad = jnp.concatenate([dot(q_t[...], d_score), dot(up_t[...], p)], axis=0)
        return dot(d_score, keys), grad

    slots[...] = jnp.zeros_like(slots)
    part, grad = backward(CHAIN, own_ref[:, :half], own_ref[:, half:])
    acc_ref[...] = part
    own_grad[...] = grad.T
    own_out = pltpu.make_async_copy(own_grad, own_any_grad, sem.at[3])
    own_out.start()

    def backward_block(b, carry):
        part, grad = backward(b, far_ref[b, :, :half], far_ref[b, :, half:])
        acc_ref[...] += part
        block = grad.astype(jnp.bfloat16).T
        if by_slot:
            slots[lineage[b]] = block
        else:
            away = lineage[b] ^ me
            kind = away % 4
            slots[away // 4 + stride * jnp.where(kind == 0, 0, jnp.where(kind == 2, 1, 2 + kind // 2))] = block
        return carry

    lax.fori_loop(0, depth, backward_block, 0)
    if by_slot:
        part_copies = [pltpu.make_async_copy(slots, parts[0].at[:, head], sem.at[6])]
    else:
        part_copies = [
            pltpu.make_async_copy(slots.at[pl.ds(stride * i, stride)], target, sem.at[6 + i])
            for i, target in enumerate([parts[0], parts[1], parts[2].at[0], parts[2].at[1]])
        ]
    for copy in part_copies:
        copy.start()
    query_grad = (acc_ref[...] * (l_ref[...] * score_scale)).astype(jnp.bfloat16)
    for h in range(heads):
        att[:, head_columns(h)] = query_grad[h * NODE_LEN : (h + 1) * NODE_LEN, :]
    dq_out = pltpu.make_async_copy(att, dq_any.at[:, pl.ds(head * width, width)], sem.at[5])
    dq_out.start()
    for copy in part_copies + [own_out]:
        copy.wait()
    proj_out.wait()
    dq_out.wait()


def attention(
    head, chunk_head, head_group, nodes, slot_heads,
    lineage, place, query_rows, own, out_grad, weight, near, old, after,
):
    bf16, f32 = jnp.bfloat16, jnp.float32
    stride = nodes // 4
    width = head_group * HEAD_DIM
    rows = head_group * NODE_LEN
    d_out = weight.shape[1]
    block = (NODE_LEN, PAIR)
    anywhere = pl.BlockSpec(memory_space=pl.ANY)
    in_smem = pl.BlockSpec(memory_space=pltpu.SMEM)
    if slot_heads:
        parts = [jax.ShapeDtypeStruct((nodes, slot_heads) + block, bf16)]
    else:
        parts = [
            jax.ShapeDtypeStruct((stride,) + block, bf16),
            jax.ShapeDtypeStruct((stride,) + block, bf16),
            jax.ShapeDtypeStruct((2, stride) + block, bf16),
        ]
    first_old = 6 + len(near)
    aliases = {first_old + i: i if i < 2 else 3 for i in range(len(old))}
    layout = (len(near), len(after), chunk_head, bool(slot_heads), len(old), head)
    blocks = (CHAIN + 1) * head_group
    return pl.pallas_call(
        functools.partial(attend, layout),
        in_specs=[in_smem, in_smem] + [anywhere] * (4 + len(near) + len(old) + len(after)),
        out_specs=[anywhere] * (3 + len(parts)),
        out_shape=[
            jax.ShapeDtypeStruct(query_rows.shape, bf16),
            jax.ShapeDtypeStruct((NODE_LEN, d_out), f32),
            jax.ShapeDtypeStruct(block, f32),
        ]
        + parts,
        input_output_aliases=aliases,
        scratch_shapes=[
            pltpu.VMEM((CHAIN,) + block, bf16),
            pltpu.VMEM(block, bf16),
            pltpu.VMEM((NODE_LEN, d_out), bf16),
            pltpu.VMEM((width, d_out), bf16),
            pltpu.VMEM((NODE_LEN, d_out), f32),
            pltpu.VMEM((NODE_LEN, width), bf16),
            pltpu.VMEM((CHAIN + 1, rows, NODE_LEN), f32),
            pltpu.VMEM((CHAIN + 1, rows, NODE_LEN), bf16),
            pltpu.VMEM((rows, HEAD_DIM), bf16),
            pltpu.VMEM((rows, HEAD_DIM), bf16),
            pltpu.VMEM((HEAD_DIM, rows), bf16),
            pltpu.VMEM((HEAD_DIM, rows), bf16),
            pltpu.VMEM((rows, HEAD_DIM), f32),
            pltpu.VMEM((rows, HEAD_DIM), f32),
            pltpu.VMEM((rows, HEAD_DIM), f32),
            pltpu.VMEM(block, f32),
            pltpu.VMEM((nodes,) + block, bf16),
            pltpu.SemaphoreType.DMA((CHAIN,)),
            pltpu.SemaphoreType.DMA((head_group,)),
            pltpu.SemaphoreType.DMA((10,)),
        ],
        compiler_params=pltpu.CompilerParams(vmem_limit_bytes=63 * 1024 * 1024),
        cost_estimate=pl.CostEstimate(
            flops=2 * blocks * NODE_LEN * NODE_LEN * HEAD_DIM,
            bytes_accessed=4 * 1024 * 1024,
            transcendentals=0,
        ),
    )(lineage, place, query_rows, own, out_grad, weight, *near, *old, *after)


def zero_of(value):
    return jnp.minimum(jnp.abs(value.astype(jnp.float32)), 0.0)


def swap(block, mask, nodes):
    return lax.ppermute(block, "node", [(i, i ^ mask) for i in range(nodes)])


def gather_near(own, nodes, zero):
    stride = nodes // 4
    line = jnp.stack([own] + [swap(own, 4 * d, nodes) for d in range(1, stride)])
    line = line + zero.astype(line.dtype)
    cross = swap(line, 2, nodes)
    return line, swap(line, 1, nodes), cross, swap(cross, 1, nodes)


def add_level_1(keep, cross, came, *refs):
    cross_sum, keep_sum = refs[-2:]
    cross_sum[...] = (cross[...].astype(jnp.float32) + came[1].astype(jnp.float32)).astype(
        jnp.bfloat16
    )
    keep_sum[...] = keep[...].astype(jnp.float32) + came[0].astype(jnp.float32)


def add_level_2(keep, came, *refs):
    keep_sum, *sent = refs[1:]
    total = keep[0] + came[0].astype(jnp.float32)
    for d in range(len(sent) + 1):

        @pl.when(pl.program_id(0) == d)
        def _():
            if d == 0:
                keep_sum[...] = total
            else:
                sent[d - 1][...] = total.astype(jnp.bfloat16)


def add_call(kernel, stride, in_specs, out_specs, out_shape, operands):
    return pl.pallas_call(
        kernel,
        grid=(stride,),
        in_specs=in_specs + [pl.BlockSpec(memory_space=pl.ANY)],
        out_specs=out_specs,
        out_shape=out_shape,
        compiler_params=pltpu.CompilerParams(vmem_limit_bytes=16 * 1024 * 1024),
        cost_estimate=pl.CostEstimate(flops=2**20, bytes_accessed=2**22, transcendentals=0),
    )(*operands)


def scatter_sum(keep, cross, away, own_part, nodes):
    bf16, f32 = jnp.bfloat16, jnp.float32
    stride = nodes // 4
    came = swap(away, 1, nodes)
    after = yield [away]
    block = keep.shape[1:]
    one = pl.BlockSpec((1,) + block, lambda d: (d, 0, 0))
    two = pl.BlockSpec((2, 1) + block, lambda d: (0, d, 0, 0))
    whole = pl.BlockSpec(block, lambda d: (0, 0))
    cross, keep = add_call(
        add_level_1,
        stride,
        [one, one, two],
        [one, one],
        [jax.ShapeDtypeStruct(cross.shape, bf16), jax.ShapeDtypeStruct(keep.shape, f32)],
        [keep, cross, came, after],
    )
    came = swap(cross, 2, nodes)
    after = yield [cross]
    keep, *sent = add_call(
        add_level_2,
        stride,
        [one, one],
        [whole] * stride,
        [jax.ShapeDtypeStruct(block, f32)] + [jax.ShapeDtypeStruct(block, bf16)] * (stride - 1),
        [keep, came, after],
    )
    came = [swap(part, 4 * (d + 1), nodes) for d, part in enumerate(sent)]
    yield sent
    total = own_part + keep
    for part in came:
        total = total + part.astype(f32)
    return total.astype(bf16)


def other_rows(block, tp):
    if tp != 2:
        whole = lax.all_gather(block, "tp", axis=0, tiled=True)
        return whole, whole
    me = lax.axis_index("tp")
    came = lax.ppermute(block, "tp", [(0, 1), (1, 0)])
    return (
        jnp.where(
            me == 0, jnp.concatenate([block, came], axis=0), jnp.concatenate([came, block], axis=0)
        ),
        came,
    )


def local(tp, nodes, query_rows, key_rows, value_rows, out_weight, out_grad, owner_slot):
    bf16, f32 = jnp.bfloat16, jnp.float32
    node_count = owner_slot.shape[0]
    tree_nodes = CHAIN + LEAVES
    kv_width = key_rows.shape[1]
    kv_heads = kv_width // HEAD_DIM
    head_group = query_rows.shape[1] // kv_width
    my_slot = lax.axis_index("node")
    numbers = jnp.arange(node_count, dtype=jnp.int32)
    tree_node = jnp.sum(jnp.where(owner_slot == my_slot, numbers, 0))
    depth = jnp.minimum(tree_node % tree_nodes, CHAIN)
    place = jnp.stack([depth, my_slot]).astype(jnp.int32)
    lineage = lax.dynamic_slice_in_dim(owner_slot, tree_node // tree_nodes * tree_nodes, CHAIN)

    out_grad_rows, came = other_rows(out_grad, tp)
    alone = min(2, kv_heads)
    chunks = [(k, 1) for k in range(alone)]
    if kv_heads > alone:
        chunks.append((alone, kv_heads - alone))
    own, near = {}, {}
    zero = zero_of(came[0, 0])
    earlier = None
    for first, heads in chunks:
        packed = []
        for k in range(first, first + heads):
            columns = slice(k * HEAD_DIM, (k + 1) * HEAD_DIM)
            packed += [key_rows[:, columns], value_rows[:, columns]]
        packed = jnp.concatenate(packed, axis=1)
        later = packed if earlier is None else packed + zero_of(earlier[0, 0, 0]).astype(bf16)
        if heads == 1:
            blocks = gather_near(later, nodes, zero)
            earlier, zero = blocks[0], zero_of(blocks[2][0, 0, 0])
        else:
            blocks = [lax.all_gather(later, "node", axis=0, tiled=False)]
        for i in range(heads):
            own[first + i], near[first + i] = (packed, i), blocks

    offloaded = max(0, kv_heads - 2)
    old, sums, own_parts = [], [], []
    sent = [earlier] if kv_heads > 1 else []
    for k in range(kv_heads):
        by_slot = k < offloaded
        dq, proj, own_part, *parts = attention(
            k, own[k][1], head_group, nodes, offloaded if by_slot else 0,
            lineage, place, query_rows, own[k][0], out_grad_rows, out_weight, near[k], old, sent,
        )
        old = [dq, proj] + (parts if k + 1 < offloaded else [])
        moved = [part for chain in sums for part in chain.send(own_part)]
        sent = moved + [own_part]
        if by_slot:
            own_parts.append(own_part)
            if k + 1 == offloaded:
                came = lax.psum_scatter(parts[0], "node", scatter_dimension=0, tiled=False)
        else:
            sums.append(scatter_sum(*parts, own_part, nodes))
            next(sums[-1])

    rows = proj.shape[0] // tp
    if tp == 2:
        me = lax.axis_index("tp")
        away = lax.dynamic_slice_in_dim(proj, (1 - me) * rows, rows, 0)
        for part in moved:
            away = away + zero_of(part[0, 0, 0])
        away = away.astype(bf16)
        here = lax.dynamic_slice_in_dim(proj, me * rows, rows, 0)
        projected = here + lax.ppermute(away, "tp", [(0, 1), (1, 0)]).astype(f32)
        projected = projected.astype(bf16)
    else:
        projected = lax.psum_scatter(proj.astype(bf16), "tp", scatter_dimension=0, tiled=True)
    moved = moved + [own_part]
    totals, steps = {}, []
    while len(totals) < len(sums):
        for n, chain in enumerate(sums):
            if n not in totals:
                try:
                    moved = chain.send(moved[0])
                    steps.append(moved[0])
                except StopIteration as end:
                    totals[n] = end.value
    totals = [totals[n] for n in range(len(sums))]
    if offloaded:
        zero = zero_of(steps[1].reshape(-1)[0])
        came = came.astype(f32) + zero
        totals = [(own_parts[k] + came[k]).astype(bf16) for k in range(offloaded)] + totals
    return (
        projected,
        dq,
        jnp.concatenate([total[:, :HEAD_DIM] for total in totals], axis=1),
        jnp.concatenate([total[:, HEAD_DIM:] for total in totals], axis=1),
    )


def solution(mesh):
    in_specs = (
        P("node", "tp"),
        P("node", "tp"),
        P("node", "tp"),
        P("tp", None),
        P(("node", "tp"), None),
        P(),
    )
    out_specs = (P(("node", "tp"), None), P("node", "tp"), P("node", "tp"), P("node", "tp"))
    return jax.shard_map(
        functools.partial(local, mesh.shape["tp"], mesh.shape["node"]),
        mesh=mesh, in_specs=in_specs, out_specs=out_specs, check_vma=False,
    )
```

```python
import functools

import jax
import jax.numpy as jnp
from jax import lax
from jax.experimental import pallas as pl
from jax.experimental.pallas import tpu as pltpu
from jax.sharding import PartitionSpec as P

HEAD_DIM = 128
NODE_LEN = 256
CHAIN = 8
LEAVES = 8
PAIR = 2 * HEAD_DIM
COLUMNS = 512

masked_score = -1e30
score_scale = HEAD_DIM ** (-0.5)
log2_e = 1.4426950408889634


def dot(a, b):
    return jnp.dot(a, b, preferred_element_type=jnp.float32)


def dot_nt(a, b):
    return lax.dot_general(a, b, (((1,), (1,)), ((), ())), preferred_element_type=jnp.float32)


def attend(layout, lineage, place, *refs):
    piece_count, near_count, after_count, chunk_head, by_slot, old_count, head = layout
    q_any, own_any, weight_any = refs[:3]
    pieces, refs = refs[3 : 3 + piece_count], refs[3 + piece_count :]
    near, refs = refs[:near_count], refs[near_count:]
    old, rest = refs[:old_count], refs[old_count + after_count :]
    dq_any, proj_any, own_any_grad = rest[:3]
    parts = rest[3 : 4 if by_slot else 5]
    (
        far_ref, own_ref, out_grad, weight, proj, att, s_ref, p_ref, qs, ups, q_t, up_t,
        m_ref, l_ref, acc_ref, own_grad, slots, far_sem, slot_sem, q_sem, piece_sem, sem,
    ) = rest[3 + len(parts) :]
    depth = place[0]
    me = place[1]
    rows = qs.shape[0]
    heads = rows // NODE_LEN
    half = HEAD_DIM
    width = heads * HEAD_DIM
    factor = score_scale * log2_e
    stride = slots.shape[0] // 4

    def head_rows(h):
        return pl.ds(h * NODE_LEN, NODE_LEN)

    def head_columns(h, first=0):
        return pl.ds(first + h * HEAD_DIM, HEAD_DIM)

    q_copies = [
        pltpu.make_async_copy(
            q_any.at[:, head_columns(h, head * width)], qs.at[head_rows(h), :], q_sem.at[h]
        )
        for h in range(heads)
    ]
    def pair_copies(source, target, sems):
        return [
            pltpu.make_async_copy(
                source.at[:, pl.ds(i * source.shape[1] // 2 + chunk_head * half, half)],
                target.at[:, pl.ds(i * half, half)],
                sems[i],
            )
            for i in range(2)
        ]

    own_copies = pair_copies(own_any, own_ref, [sem.at[0], sem.at[2]])
    weight_copy = pltpu.make_async_copy(
        weight_any.at[pl.ds(head * width, width), :], weight, sem.at[1]
    )
    piece_rows = pieces[0].shape[0]
    piece_copies = [
        pltpu.make_async_copy(
            piece,
            out_grad.at[pl.ds(pl.multiple_of((place[2] ^ i) * piece_rows, piece_rows), piece_rows), :],
            piece_sem.at[i],
        )
        for i, piece in enumerate(pieces)
    ]
    for copy in own_copies + q_copies:
        copy.start()

    def far_copies(source, index, b):
        return pair_copies(
            source.at[index], far_ref.at[b], [far_sem.at[b], far_sem.at[CHAIN + b]]
        )

    def fetch(b, carry):
        if near_count == 1:
            for copy in far_copies(near[0], lineage[b], b):
                copy.start()
            return carry
        away = lineage[b] ^ me
        for kind in range(near_count):

            @pl.when(away % 4 == kind)
            def _():
                for copy in far_copies(near[kind], away // 4, b):
                    copy.start()

        return carry

    lax.fori_loop(0, depth, fetch, 0)
    weight_copy.start()
    for copy in piece_copies:
        copy.start()
    if head > 0:
        proj_copy = pltpu.make_async_copy(old[1], proj, sem.at[3])
        proj_copy.start()

    def fold_max(s):
        return jnp.maximum(s[:, :half], s[:, half:])

    for copy in own_copies + q_copies:
        copy.wait()
    s = dot_nt(qs[...], own_ref[:, :half])
    row = lax.broadcasted_iota(jnp.int32, (rows, NODE_LEN), 0) % NODE_LEN
    col = lax.broadcasted_iota(jnp.int32, (rows, NODE_LEN), 1)
    s = jnp.where(col <= row, s, masked_score)
    s_ref[CHAIN] = s
    m_ref[...] = fold_max(s)

    def score_block(b, carry):
        for copy in far_copies(near[0], 0, b):
            copy.wait()
        s = dot_nt(qs[...], far_ref[b, :, :half])
        s_ref[b] = s
        m_ref[...] = jnp.maximum(m_ref[...], fold_max(s))
        return carry

    lax.fori_loop(0, depth, score_block, 0)
    m_ref[...] = jnp.broadcast_to(jnp.max(m_ref[...], axis=1, keepdims=True), (rows, half))

    def weigh(b, values):
        top = m_ref[...]
        s = s_ref[b]
        p_low = jnp.exp2((s[:, :half] - top) * factor)
        p_high = jnp.exp2((s[:, half:] - top) * factor)
        p = jnp.concatenate([p_low, p_high], axis=1).astype(jnp.bfloat16)
        p_ref[b] = p
        return p_low + p_high, dot(p, values)

    part_sum, part = weigh(CHAIN, own_ref[:, half:])
    l_ref[...] = part_sum
    acc_ref[...] = part

    def forward_block(b, carry):
        part_sum, part = weigh(b, far_ref[b, :, half:])
        l_ref[...] += part_sum
        acc_ref[...] += part
        return carry

    lax.fori_loop(0, depth, forward_block, 0)
    inverse = 1.0 / jnp.broadcast_to(jnp.sum(l_ref[...], axis=1, keepdims=True), (rows, half))
    l_ref[...] = inverse
    attended = (acc_ref[...] * inverse).astype(jnp.bfloat16)
    for h in range(heads):
        att[:, head_columns(h)] = attended[h * NODE_LEN : (h + 1) * NODE_LEN, :]

    weight_copy.wait()
    for copy in piece_copies:
        copy.wait()
    for h in range(0, heads, 2):
        count = min(2, heads - h)
        two = dot_nt(out_grad[...], weight[h * HEAD_DIM : (h + count) * HEAD_DIM, :])
        for i in range(count):
            ups[head_rows(h + i), :] = two[:, i * HEAD_DIM : (i + 1) * HEAD_DIM].astype(jnp.bfloat16)
    if head > 0:
        proj_copy.wait()

    def project(n, carry):
        columns = pl.ds(pl.multiple_of(n * COLUMNS, COLUMNS), COLUMNS)
        share = dot(att[...], weight[:, columns])
        proj[:, columns] = share if head == 0 else proj[:, columns] + share
        return carry

    lax.fori_loop(0, weight.shape[1] // COLUMNS, project, 0)
    proj_out = pltpu.make_async_copy(proj, proj_any, sem.at[4])
    proj_out.start()

    upstream = ups[...].astype(jnp.float32)
    corr_ref = m_ref
    corr_ref[...] = jnp.broadcast_to(
        jnp.sum(upstream * attended.astype(jnp.float32), axis=1, keepdims=True), (rows, half)
    )
    q_t[...] = (qs[...].astype(jnp.float32) * (inverse * score_scale)).astype(jnp.bfloat16).T
    up_t[...] = (upstream * inverse).astype(jnp.bfloat16).T

    def backward(b, keys, values):
        corr = corr_ref[...]
        p = p_ref[b]
        d_prob = dot_nt(ups[...], values)
        centred = jnp.concatenate([d_prob[:, :half] - corr, d_prob[:, half:] - corr], axis=1)
        d_score = (p.astype(jnp.float32) * centred).astype(jnp.bfloat16)
        grad = jnp.concatenate([dot(q_t[...], d_score), dot(up_t[...], p)], axis=0)
        return dot(d_score, keys), grad

    def slot_place(b):
        if by_slot:
            return lineage[b]
        away = lineage[b] ^ me
        kind = away % 4
        return away // 4 + stride * jnp.where(kind == 0, 0, jnp.where(kind == 2, 1, 2 + kind // 2))

    def slot_copy(slot, target):
        return pltpu.make_async_copy(slots.at[slot], target, slot_sem.at[slot])

    def send_out(slot):
        if by_slot:
            slot_copy(slot, parts[0].at[slot, head]).start()
            return

        @pl.when(slot < 2 * stride)
        def _():
            slot_copy(slot, parts[0].at[slot]).start()

        @pl.when(slot >= 2 * stride)
        def _():
            slot_copy(slot, parts[1].at[slot - 2 * stride]).start()

    def is_far(slot):
        return functools.reduce(
            jnp.logical_or, [jnp.logical_and(b < depth, slot_place(b) == slot) for b in range(CHAIN)]
        )

    def clear(slot, carry):
        @pl.when(jnp.logical_not(is_far(slot)))
        def _():
            slots[slot] = jnp.zeros(slots.shape[1:], slots.dtype)
            send_out(slot)

        return carry

    lax.fori_loop(0, slots.shape[0], clear, 0)
    part, grad = backward(CHAIN, own_ref[:, :half], own_ref[:, half:])
    acc_ref[...] = part
    own_grad[...] = grad.T
    own_out = pltpu.make_async_copy(own_grad, own_any_grad, sem.at[3])
    own_out.start()

    def backward_block(b, carry):
        part, grad = backward(b, far_ref[b, :, :half], far_ref[b, :, half:])
        acc_ref[...] += part
        block = grad.astype(jnp.bfloat16).T
        slot = slot_place(b)
        slots[slot] = block
        send_out(slot)
        return carry

    lax.fori_loop(0, depth, backward_block, 0)
    query_grad = (acc_ref[...] * (l_ref[...] * score_scale)).astype(jnp.bfloat16)
    for h in range(heads):
        att[:, head_columns(h)] = query_grad[h * NODE_LEN : (h + 1) * NODE_LEN, :]
    dq_out = pltpu.make_async_copy(att, dq_any.at[:, pl.ds(head * width, width)], sem.at[5])
    dq_out.start()
    own_out.wait()

    def finish(slot, carry):
        slot_copy(slot, parts[0].at[0, head] if by_slot else parts[0].at[0]).wait()
        return carry

    lax.fori_loop(0, slots.shape[0], finish, 0)
    proj_out.wait()
    dq_out.wait()


def attention(
    head, chunk_head, head_group, nodes, slot_heads,
    lineage, place, query_rows, own, weight, pieces, near, old, after,
):
    bf16, f32 = jnp.bfloat16, jnp.float32
    stride = nodes // 4
    width = head_group * HEAD_DIM
    rows = head_group * NODE_LEN
    d_out = weight.shape[1]
    block = (NODE_LEN, PAIR)
    anywhere = pl.BlockSpec(memory_space=pl.ANY)
    in_smem = pl.BlockSpec(memory_space=pltpu.SMEM)
    if slot_heads:
        parts = [jax.ShapeDtypeStruct((nodes, slot_heads) + block, bf16)]
    else:
        parts = [jax.ShapeDtypeStruct((2 * stride,) + block, bf16)] * 2
    first_old = 5 + len(pieces) + len(near)
    aliases = {first_old + i: i if i < 2 else 3 for i in range(len(old))}
    layout = (len(pieces), len(near), len(after), chunk_head, bool(slot_heads), len(old), head)
    blocks = (CHAIN + 1) * head_group
    return pl.pallas_call(
        functools.partial(attend, layout),
        in_specs=[in_smem, in_smem] + [anywhere] * (3 + len(pieces) + len(near) + len(old) + len(after)),
        out_specs=[anywhere] * (3 + len(parts)),
        out_shape=[
            jax.ShapeDtypeStruct(query_rows.shape, bf16),
            jax.ShapeDtypeStruct((NODE_LEN, d_out), f32),
            jax.ShapeDtypeStruct(block, f32),
        ]
        + parts,
        input_output_aliases=aliases,
        scratch_shapes=[
            pltpu.VMEM((CHAIN,) + block, bf16),
            pltpu.VMEM(block, bf16),
            pltpu.VMEM((NODE_LEN, d_out), bf16),
            pltpu.VMEM((width, d_out), bf16),
            pltpu.VMEM((NODE_LEN, d_out), f32),
            pltpu.VMEM((NODE_LEN, width), bf16),
            pltpu.VMEM((CHAIN + 1, rows, NODE_LEN), f32),
            pltpu.VMEM((CHAIN + 1, rows, NODE_LEN), bf16),
            pltpu.VMEM((rows, HEAD_DIM), bf16),
            pltpu.VMEM((rows, HEAD_DIM), bf16),
            pltpu.VMEM((HEAD_DIM, rows), bf16),
            pltpu.VMEM((HEAD_DIM, rows), bf16),
            pltpu.VMEM((rows, HEAD_DIM), f32),
            pltpu.VMEM((rows, HEAD_DIM), f32),
            pltpu.VMEM((rows, HEAD_DIM), f32),
            pltpu.VMEM(block, f32),
            pltpu.VMEM((nodes,) + block, bf16),
            pltpu.SemaphoreType.DMA((2 * CHAIN,)),
            pltpu.SemaphoreType.DMA((nodes,)),
            pltpu.SemaphoreType.DMA((head_group,)),
            pltpu.SemaphoreType.DMA((2,)),
            pltpu.SemaphoreType.DMA((6,)),
        ],
        compiler_params=pltpu.CompilerParams(vmem_limit_bytes=63 * 1024 * 1024),
        cost_estimate=pl.CostEstimate(
            flops=2 * blocks * NODE_LEN * NODE_LEN * HEAD_DIM,
            bytes_accessed=4 * 1024 * 1024,
            transcendentals=0,
        ),
    )(lineage, place, query_rows, own, weight, *pieces, *near, *old, *after)


def zero_of(value):
    return jnp.minimum(jnp.abs(value.astype(jnp.float32)), 0.0)


def swap(block, mask, nodes):
    return lax.ppermute(block, "node", [(i, i ^ mask) for i in range(nodes)])


def gather_near(own, nodes):
    stride = nodes // 4
    line = jnp.stack([own] + [swap(own, 4 * d, nodes) for d in range(1, stride)])
    cross = swap(line, 2, nodes)
    return [line, swap(line, 1, nodes), cross, swap(cross, 1, nodes)]


def add_level_1(keep, cross, came_keep, came_cross, after, cross_sum, keep_sum):
    f32 = jnp.float32
    cross_sum[...] = (cross[...].astype(f32) + came_cross[...].astype(f32)).astype(jnp.bfloat16)
    keep_sum[...] = keep[...].astype(f32) + came_keep[...].astype(f32)


def add_level_2(keep, came, *refs):
    keep_sum, *sent = refs[1:]
    total = keep[0] + came[0].astype(jnp.float32)
    for d in range(len(sent) + 1):

        @pl.when(pl.program_id(0) == d)
        def _():
            if d == 0:
                keep_sum[...] = total
            else:
                sent[d - 1][...] = total.astype(jnp.bfloat16)


def add_call(kernel, stride, in_specs, out_specs, out_shape, operands):
    return pl.pallas_call(
        kernel,
        grid=(stride,),
        in_specs=in_specs + [pl.BlockSpec(memory_space=pl.ANY)],
        out_specs=out_specs,
        out_shape=out_shape,
        compiler_params=pltpu.CompilerParams(vmem_limit_bytes=16 * 1024 * 1024),
        cost_estimate=pl.CostEstimate(flops=2**20, bytes_accessed=2**22, transcendentals=0),
    )(*operands)


def scatter_sum(kept, away, own_part, nodes):
    bf16, f32 = jnp.bfloat16, jnp.float32
    stride = nodes // 4
    came = swap(away, 1, nodes)
    after = yield [away]
    block = kept.shape[1:]
    one = pl.BlockSpec((1,) + block, lambda d: (d, 0, 0))
    far = pl.BlockSpec((1,) + block, lambda d: (stride + d, 0, 0))
    whole = pl.BlockSpec(block, lambda d: (0, 0))
    cross, keep = add_call(
        add_level_1,
        stride,
        [one, far, one, far],
        [one, one],
        [jax.ShapeDtypeStruct((stride,) + block, t) for t in (bf16, f32)],
        [kept, kept, came, came, after],
    )
    came = swap(cross, 2, nodes)
    after = yield [cross]
    keep, *sent = add_call(
        add_level_2,
        stride,
        [one, one],
        [whole] * stride,
        [jax.ShapeDtypeStruct(block, f32)] + [jax.ShapeDtypeStruct(block, bf16)] * (stride - 1),
        [keep, came, after],
    )
    came = [swap(part, 4 * (d + 1), nodes) for d, part in enumerate(sent)]
    after = yield sent
    total = own_part + (keep + zero_of(after.reshape(-1)[0]))
    for part in came:
        total = total + part.astype(f32)
    return total.astype(bf16)


def local(tp, nodes, query_rows, key_rows, value_rows, out_weight, out_grad, owner_slot):
    bf16, f32 = jnp.bfloat16, jnp.float32
    node_count = owner_slot.shape[0]
    tree_nodes = CHAIN + LEAVES
    kv_width = key_rows.shape[1]
    kv_heads = kv_width // HEAD_DIM
    head_group = query_rows.shape[1] // kv_width
    my_slot = lax.axis_index("node")
    numbers = jnp.arange(node_count, dtype=jnp.int32)
    tree_node = jnp.sum(jnp.where(owner_slot == my_slot, numbers, 0))
    depth = jnp.minimum(tree_node % tree_nodes, CHAIN)
    order = lax.axis_index("tp") if tp == 2 else 0
    place = jnp.stack([depth, my_slot, order]).astype(jnp.int32)
    lineage = lax.dynamic_slice_in_dim(owner_slot, tree_node // tree_nodes * tree_nodes, CHAIN)

    if tp == 2:
        pieces = [out_grad, lax.ppermute(out_grad, "tp", [(0, 1), (1, 0)])]
    else:
        pieces = [lax.all_gather(out_grad, "tp", axis=0, tiled=True)]

    own, near = {}, {}
    chunks = [(0, 1), (1, 1), (2, kv_heads - 2)]
    for first, heads in [chunk for chunk in chunks if chunk[0] < kv_heads]:
        columns = slice(first * HEAD_DIM, (first + heads) * HEAD_DIM)
        packed = jnp.concatenate([key_rows[:, columns], value_rows[:, columns]], axis=1)
        if first == 0:
            blocks = gather_near(packed, nodes)
        else:
            if first > 1:
                for value in near[0][1:] + near[1] + pieces[1:]:
                    packed = packed + zero_of(value.reshape(-1)[0]).astype(bf16)
            blocks = [lax.all_gather(packed, "node", axis=0, tiled=False)]
        for i in range(heads):
            own[first + i], near[first + i] = (packed, i), blocks

    offloaded = max(0, kv_heads - 2)
    old, sums, own_parts = [], [], []
    sent = near[1] if kv_heads > 1 else []
    for k in range(kv_heads):
        by_slot = k < offloaded
        dq, proj, own_part, *parts = attention(
            k, own[k][1], head_group, nodes, offloaded if by_slot else 0,
            lineage, place, query_rows, own[k][0], out_weight, pieces, near[k], old, sent,
        )
        old = [dq, proj] + (parts if k + 1 < offloaded else [])
        sent = [own_part]
        if by_slot:
            own_parts.append(own_part)
            if k + 1 == offloaded:
                came = lax.psum_scatter(parts[0], "node", scatter_dimension=0, tiled=False)
        else:
            sums.append(scatter_sum(*parts, own_part, nodes))
            sent = next(sums[-1])
            if k + 1 < kv_heads:
                sent = sums[-1].send(own_part)

    *earlier, last = sums
    early = [chain.send(own_part)[0] for chain in earlier] + [own_part]
    middle = last.send(early[0])[0]
    rows = proj.shape[0] // tp
    if tp == 2:
        me = lax.axis_index("tp")
        away = lax.dynamic_slice_in_dim(proj, (1 - me) * rows, rows, 0)
        away = (away + zero_of(early[0].reshape(-1)[0])).astype(bf16)
        here = lax.dynamic_slice_in_dim(proj, me * rows, rows, 0)
        projected = here + lax.ppermute(away, "tp", [(0, 1), (1, 0)]).astype(f32)
        projected = projected.astype(bf16)
    else:
        projected = lax.psum_scatter(proj.astype(bf16), "tp", scatter_dimension=0, tiled=True)
    moved = last.send(middle)[0]
    totals = []
    for chain in earlier + [last]:
        try:
            chain.send(moved)
        except StopIteration as end:
            totals.append(end.value)
    if offloaded:
        came = came.astype(f32) + zero_of(middle.reshape(-1)[0])
        totals = [(own_parts[k] + came[k]).astype(bf16) for k in range(offloaded)] + totals
    return (
        projected,
        dq,
        jnp.concatenate([total[:, :HEAD_DIM] for total in totals], axis=1),
        jnp.concatenate([total[:, HEAD_DIM:] for total in totals], axis=1),
    )


def solution(mesh):
    in_specs = (
        P("node", "tp"),
        P("node", "tp"),
        P("node", "tp"),
        P("tp", None),
        P(("node", "tp"), None),
        P(),
    )
    out_specs = (P(("node", "tp"), None), P("node", "tp"), P("node", "tp"), P("node", "tp"))
    return jax.shard_map(
        functools.partial(local, mesh.shape["tp"], mesh.shape["node"]),
        mesh=mesh, in_specs=in_specs, out_specs=out_specs, check_vma=False,
    )
```

```python
import functools

import jax
import jax.numpy as jnp
from jax import lax
from jax.experimental import pallas as pl
from jax.experimental.pallas import tpu as pltpu
from jax.sharding import PartitionSpec as P

HEAD_DIM = 128
NODE_LEN = 256
CHAIN = 8
LEAVES = 8
PAIR = 2 * HEAD_DIM
COLUMNS = 512

masked_score = -1e30
score_scale = HEAD_DIM ** (-0.5)
log2_e = 1.4426950408889634


def dot(a, b):
    return jnp.dot(a, b, preferred_element_type=jnp.float32)


def dot_nt(a, b):
    return lax.dot_general(a, b, (((1,), (1,)), ((), ())), preferred_element_type=jnp.float32)


def attend(layout, owner_slot, *refs):
    piece_count, near_count, after_count, chunk_head, by_slot, old_count, head = layout
    q_any, own_any, weight_any = refs[:3]
    pieces, refs = refs[3 : 3 + piece_count], refs[3 + piece_count :]
    near, refs = refs[:near_count], refs[near_count:]
    old, rest = refs[:old_count], refs[old_count + after_count :]
    dq_any, proj_any, own_any_grad = rest[:3]
    parts = rest[3 : 4 if by_slot else 5]
    (
        far_ref, own_ref, out_grad, weight, proj, att, s_ref, p_ref, qs, ups, q_t, up_t,
        m_ref, l_ref, acc_ref, own_grad, slots, far_sem, slot_sem, q_sem, piece_sem, sem,
    ) = rest[3 + len(parts) :]
    me = lax.axis_index("node")
    node_count = owner_slot.shape[0]
    tree_node = jnp.int32(0)
    for n in range(node_count):
        tree_node = jnp.where(owner_slot[n] == me, n, tree_node)
    tree_nodes = CHAIN + LEAVES
    first_node = tree_node // tree_nodes * tree_nodes
    depth = jnp.minimum(tree_node - first_node, CHAIN)
    lineage = [owner_slot[first_node + b] for b in range(CHAIN)]

    def ancestor(b):
        return lineage[b] if isinstance(b, int) else owner_slot[first_node + b]

    rows = qs.shape[0]
    heads = rows // NODE_LEN
    half = HEAD_DIM
    width = heads * HEAD_DIM
    factor = score_scale * log2_e
    stride = slots.shape[0] // 4

    def head_rows(h):
        return pl.ds(h * NODE_LEN, NODE_LEN)

    def head_columns(h, first=0):
        return pl.ds(first + h * HEAD_DIM, HEAD_DIM)

    q_copies = [
        pltpu.make_async_copy(
            q_any.at[:, head_columns(h, head * width)], qs.at[head_rows(h), :], q_sem.at[h]
        )
        for h in range(heads)
    ]
    def pair_copies(source, target, sems):
        return [
            pltpu.make_async_copy(
                source.at[:, pl.ds(i * source.shape[1] // 2 + chunk_head * half, half)],
                target.at[:, pl.ds(i * half, half)],
                sems[i],
            )
            for i in range(2)
        ]

    own_copies = pair_copies(own_any, own_ref, [sem.at[0], sem.at[2]])
    weight_copy = pltpu.make_async_copy(
        weight_any.at[pl.ds(head * width, width), :], weight, sem.at[1]
    )
    order = lax.axis_index("tp") if piece_count == 2 else 0
    piece_rows = pieces[0].shape[0]
    piece_copies = [
        pltpu.make_async_copy(
            piece,
            out_grad.at[pl.ds(pl.multiple_of((order ^ i) * piece_rows, piece_rows), piece_rows), :],
            piece_sem.at[i],
        )
        for i, piece in enumerate(pieces)
    ]
    for copy in own_copies + q_copies:
        copy.start()

    def far_copies(source, index, b):
        return pair_copies(
            source.at[index], far_ref.at[b], [far_sem.at[b], far_sem.at[CHAIN + b]]
        )

    def fetch(b, carry):
        if near_count == 1:
            for copy in far_copies(near[0], ancestor(b), b):
                copy.start()
            return carry
        away = ancestor(b) ^ me
        for kind in range(near_count):

            @pl.when(away % 4 == kind)
            def _():
                for copy in far_copies(near[kind], away // 4, b):
                    copy.start()

        return carry

    lax.fori_loop(0, depth, fetch, 0)

    def fold_max(s):
        return jnp.maximum(s[:, :half], s[:, half:])

    for copy in own_copies + q_copies:
        copy.wait()
    s = dot_nt(qs[...], own_ref[:, :half])
    row = lax.broadcasted_iota(jnp.int32, (rows, NODE_LEN), 0) % NODE_LEN
    col = lax.broadcasted_iota(jnp.int32, (rows, NODE_LEN), 1)
    s = jnp.where(col <= row, s, masked_score)
    s_ref[CHAIN] = s
    m_ref[...] = fold_max(s)

    def score_block(b, carry):
        for copy in far_copies(near[0], 0, b):
            copy.wait()
        s = dot_nt(qs[...], far_ref[b, :, :half])
        s_ref[b] = s
        m_ref[...] = jnp.maximum(m_ref[...], fold_max(s))
        return carry

    lax.fori_loop(0, depth, score_block, 0)

    late_copies = [weight_copy] + piece_copies
    if head > 0:
        late_copies.append(pltpu.make_async_copy(old[1], proj, sem.at[3]))
    for copy in late_copies:
        copy.start()
    m_ref[...] = jnp.broadcast_to(jnp.max(m_ref[...], axis=1, keepdims=True), (rows, half))

    def weigh(b, values):
        top = m_ref[...]
        s = s_ref[b]
        p_low = jnp.exp2((s[:, :half] - top) * factor)
        p_high = jnp.exp2((s[:, half:] - top) * factor)
        p = jnp.concatenate([p_low, p_high], axis=1).astype(jnp.bfloat16)
        p_ref[b] = p
        return p_low + p_high, dot(p, values)

    part_sum, part = weigh(CHAIN, own_ref[:, half:])
    l_ref[...] = part_sum
    acc_ref[...] = part

    def forward_block(b, carry):
        part_sum, part = weigh(b, far_ref[b, :, half:])
        l_ref[...] += part_sum
        acc_ref[...] += part
        return carry

    lax.fori_loop(0, depth, forward_block, 0)
    inverse = 1.0 / jnp.broadcast_to(jnp.sum(l_ref[...], axis=1, keepdims=True), (rows, half))
    l_ref[...] = inverse
    attended = (acc_ref[...] * inverse).astype(jnp.bfloat16)
    for h in range(heads):
        att[:, head_columns(h)] = attended[h * NODE_LEN : (h + 1) * NODE_LEN, :]

    for copy in late_copies:
        copy.wait()
    for h in range(0, heads, 2):
        count = min(2, heads - h)
        two = dot_nt(out_grad[...], weight[h * HEAD_DIM : (h + count) * HEAD_DIM, :])
        for i in range(count):
            ups[head_rows(h + i), :] = two[:, i * HEAD_DIM : (i + 1) * HEAD_DIM].astype(jnp.bfloat16)

    def project(n, carry):
        columns = pl.ds(pl.multiple_of(n * COLUMNS, COLUMNS), COLUMNS)
        share = dot(att[...], weight[:, columns])
        proj[:, columns] = share if head == 0 else proj[:, columns] + share
        return carry

    lax.fori_loop(0, weight.shape[1] // COLUMNS, project, 0)
    proj_out = pltpu.make_async_copy(proj, proj_any, sem.at[4])
    proj_out.start()

    upstream = ups[...].astype(jnp.float32)
    corr_ref = m_ref
    corr_ref[...] = jnp.broadcast_to(
        jnp.sum(upstream * attended.astype(jnp.float32), axis=1, keepdims=True), (rows, half)
    )
    q_t[...] = (qs[...].astype(jnp.float32) * (inverse * score_scale)).astype(jnp.bfloat16).T
    up_t[...] = (upstream * inverse).astype(jnp.bfloat16).T

    def backward(b, keys, values):
        corr = corr_ref[...]
        p = p_ref[b]
        d_prob = dot_nt(ups[...], values)
        centred = jnp.concatenate([d_prob[:, :half] - corr, d_prob[:, half:] - corr], axis=1)
        d_score = (p.astype(jnp.float32) * centred).astype(jnp.bfloat16)
        grad = jnp.concatenate([dot(q_t[...], d_score), dot(up_t[...], p)], axis=0)
        return dot(d_score, keys), grad

    def slot_place(b):
        if by_slot:
            return ancestor(b)
        away = ancestor(b) ^ me
        kind = away % 4
        return away // 4 + stride * jnp.where(kind == 0, 0, jnp.where(kind == 2, 1, 2 + kind // 2))

    def slot_copy(slot, target):
        return pltpu.make_async_copy(slots.at[slot], target, slot_sem.at[slot])

    def send_out(slot):
        if by_slot:
            slot_copy(slot, parts[0].at[slot, head]).start()
            return

        @pl.when(slot < 2 * stride)
        def _():
            slot_copy(slot, parts[0].at[slot]).start()

        @pl.when(slot >= 2 * stride)
        def _():
            slot_copy(slot, parts[1].at[slot - 2 * stride]).start()

    def is_far(slot):
        return functools.reduce(
            jnp.logical_or, [jnp.logical_and(b < depth, slot_place(b) == slot) for b in range(CHAIN)]
        )

    def clear(slot, carry):
        @pl.when(jnp.logical_not(is_far(slot)))
        def _():
            slots[slot] = jnp.zeros(slots.shape[1:], slots.dtype)
            send_out(slot)

        return carry

    lax.fori_loop(0, slots.shape[0], clear, 0)
    part, grad = backward(CHAIN, own_ref[:, :half], own_ref[:, half:])
    acc_ref[...] = part
    own_grad[...] = grad.T
    own_out = pltpu.make_async_copy(own_grad, own_any_grad, sem.at[3])
    own_out.start()

    def backward_block(b, carry):
        part, grad = backward(b, far_ref[b, :, :half], far_ref[b, :, half:])
        acc_ref[...] += part
        block = grad.astype(jnp.bfloat16).T
        slot = slot_place(b)
        slots[slot] = block
        send_out(slot)
        return carry

    lax.fori_loop(0, depth, backward_block, 0)
    query_grad = (acc_ref[...] * (l_ref[...] * score_scale)).astype(jnp.bfloat16)
    for h in range(heads):
        att[:, head_columns(h)] = query_grad[h * NODE_LEN : (h + 1) * NODE_LEN, :]
    dq_out = pltpu.make_async_copy(att, dq_any.at[:, pl.ds(head * width, width)], sem.at[5])
    dq_out.start()
    own_out.wait()

    def finish(slot, carry):
        slot_copy(slot, parts[0].at[0, head] if by_slot else parts[0].at[0]).wait()
        return carry

    lax.fori_loop(0, slots.shape[0], finish, 0)
    proj_out.wait()
    dq_out.wait()


def attention(
    head, chunk_head, head_group, nodes, slot_heads,
    owner_slot, query_rows, own, weight, pieces, near, old, after,
):
    bf16, f32 = jnp.bfloat16, jnp.float32
    stride = nodes // 4
    width = head_group * HEAD_DIM
    rows = head_group * NODE_LEN
    d_out = weight.shape[1]
    block = (NODE_LEN, PAIR)
    anywhere = pl.BlockSpec(memory_space=pl.ANY)
    in_smem = pl.BlockSpec(memory_space=pltpu.SMEM)
    if slot_heads:
        parts = [jax.ShapeDtypeStruct((nodes, slot_heads) + block, bf16)]
    else:
        parts = [jax.ShapeDtypeStruct((2 * stride,) + block, bf16)] * 2
    first_old = 4 + len(pieces) + len(near)
    aliases = {first_old + i: i if i < 2 else 3 for i in range(len(old))}
    layout = (len(pieces), len(near), len(after), chunk_head, bool(slot_heads), len(old), head)
    blocks = (CHAIN + 1) * head_group
    return pl.pallas_call(
        functools.partial(attend, layout),
        in_specs=[in_smem] + [anywhere] * (3 + len(pieces) + len(near) + len(old) + len(after)),
        out_specs=[anywhere] * (3 + len(parts)),
        out_shape=[
            jax.ShapeDtypeStruct(query_rows.shape, bf16),
            jax.ShapeDtypeStruct((NODE_LEN, d_out), f32),
            jax.ShapeDtypeStruct(block, f32),
        ]
        + parts,
        input_output_aliases=aliases,
        scratch_shapes=[
            pltpu.VMEM((CHAIN,) + block, bf16),
            pltpu.VMEM(block, bf16),
            pltpu.VMEM((NODE_LEN, d_out), bf16),
            pltpu.VMEM((width, d_out), bf16),
            pltpu.VMEM((NODE_LEN, d_out), f32),
            pltpu.VMEM((NODE_LEN, width), bf16),
            pltpu.VMEM((CHAIN + 1, rows, NODE_LEN), f32),
            pltpu.VMEM((CHAIN + 1, rows, NODE_LEN), bf16),
            pltpu.VMEM((rows, HEAD_DIM), bf16),
            pltpu.VMEM((rows, HEAD_DIM), bf16),
            pltpu.VMEM((HEAD_DIM, rows), bf16),
            pltpu.VMEM((HEAD_DIM, rows), bf16),
            pltpu.VMEM((rows, HEAD_DIM), f32),
            pltpu.VMEM((rows, HEAD_DIM), f32),
            pltpu.VMEM((rows, HEAD_DIM), f32),
            pltpu.VMEM(block, f32),
            pltpu.VMEM((nodes,) + block, bf16),
            pltpu.SemaphoreType.DMA((2 * CHAIN,)),
            pltpu.SemaphoreType.DMA((nodes,)),
            pltpu.SemaphoreType.DMA((head_group,)),
            pltpu.SemaphoreType.DMA((2,)),
            pltpu.SemaphoreType.DMA((6,)),
        ],
        compiler_params=pltpu.CompilerParams(vmem_limit_bytes=63 * 1024 * 1024),
        cost_estimate=pl.CostEstimate(
            flops=2 * blocks * NODE_LEN,
            bytes_accessed=2**20,
            transcendentals=0,
        ),
    )(owner_slot, query_rows, own, weight, *pieces, *near, *old, *after)


def swap(block, mask, nodes):
    return lax.ppermute(block, "node", [(i, i ^ mask) for i in range(nodes)])


def gather_near(own, nodes):
    stride = nodes // 4
    line = jnp.stack([own] + [swap(own, 4 * d, nodes) for d in range(1, stride)])
    cross = swap(line, 2, nodes)
    return [line, swap(line, 1, nodes), cross, swap(cross, 1, nodes)]


def add_level_1(keep, cross, came_keep, came_cross, after, cross_sum, keep_sum):
    f32 = jnp.float32
    cross_sum[...] = (cross[...].astype(f32) + came_cross[...].astype(f32)).astype(jnp.bfloat16)
    keep_sum[...] = keep[...].astype(f32) + came_keep[...].astype(f32)


def add_level_2(keep, came, *refs):
    keep_sum, *sent = refs[1:]
    total = keep[0] + came[0].astype(jnp.float32)
    for d in range(len(sent) + 1):

        @pl.when(pl.program_id(0) == d)
        def _():
            if d == 0:
                keep_sum[...] = total
            else:
                sent[d - 1][...] = total.astype(jnp.bfloat16)


def add_all(*refs):
    *parts, after, total = refs
    total[...] = functools.reduce(
        jnp.add, [part[...].reshape(total.shape).astype(jnp.float32) for part in parts]
    ).astype(total.dtype)


def copy_out(rows, after, out):
    out[...] = rows[...].astype(out.dtype)


def small_call(kernel, grid, in_specs, out_specs, out_shape, operands, after):
    return pl.pallas_call(
        kernel,
        grid=grid,
        in_specs=in_specs + [pl.BlockSpec(memory_space=pl.ANY)],
        out_specs=out_specs,
        out_shape=out_shape,
        compiler_params=pltpu.CompilerParams(vmem_limit_bytes=63 * 1024 * 1024),
        cost_estimate=pl.CostEstimate(flops=2**10, bytes_accessed=2**12, transcendentals=0),
    )(*operands, after)


def final_sum(parts, after):
    block = parts[0].shape[-2:]
    out = pl.BlockSpec(block, lambda i: (0, 0))
    specs = [
        pl.BlockSpec(part.shape, lambda i, n=part.ndim: (0,) * n) for part in parts
    ]
    return small_call(
        add_all, (1,), specs, out, jax.ShapeDtypeStruct(block, jnp.bfloat16), parts, after
    )


def scatter_sum(kept, away, own_part, nodes):
    bf16, f32 = jnp.bfloat16, jnp.float32
    stride = nodes // 4
    came = swap(away, 1, nodes)
    after = yield [away]
    block = kept.shape[1:]
    one = pl.BlockSpec((1,) + block, lambda d: (d, 0, 0))
    far = pl.BlockSpec((1,) + block, lambda d: (stride + d, 0, 0))
    whole = pl.BlockSpec(block, lambda d: (0, 0))
    cross, keep = small_call(
        add_level_1,
        (stride,),
        [one, far, one, far],
        [one, one],
        [jax.ShapeDtypeStruct((stride,) + block, t) for t in (bf16, f32)],
        [kept, kept, came, came],
        after,
    )
    came = swap(cross, 2, nodes)
    after = yield [cross]
    keep, *sent = small_call(
        add_level_2,
        (stride,),
        [one, one],
        [whole] * stride,
        [jax.ShapeDtypeStruct(block, f32)] + [jax.ShapeDtypeStruct(block, bf16)] * (stride - 1),
        [keep, came],
        after,
    )
    came = [swap(part, 4 * (d + 1), nodes) for d, part in enumerate(sent)]
    after = yield sent
    return final_sum([own_part, keep] + came, after)


def local(tp, nodes, query_rows, key_rows, value_rows, out_weight, out_grad, owner_slot):
    bf16, f32 = jnp.bfloat16, jnp.float32
    kv_width = key_rows.shape[1]
    kv_heads = kv_width // HEAD_DIM
    head_group = query_rows.shape[1] // kv_width
    if tp == 2:
        pieces = [out_grad, lax.ppermute(out_grad, "tp", [(0, 1), (1, 0)])]
    else:
        pieces = [lax.all_gather(out_grad, "tp", axis=0, tiled=True)]

    own, near = {}, {}
    for first, heads in [(0, 1)] + ([(1, kv_heads - 1)] if kv_heads > 1 else []):
        columns = slice(first * HEAD_DIM, (first + heads) * HEAD_DIM)
        packed = jnp.concatenate([key_rows[:, columns], value_rows[:, columns]], axis=1)
        if first == 0:
            blocks = gather_near(packed, nodes)
        else:
            blocks = [lax.all_gather(packed, "node", axis=0, tiled=False)]
        for i in range(heads):
            own[first + i], near[first + i] = (packed, i), blocks

    offloaded = max(0, kv_heads - 2)
    old, sums, own_parts, sent = [], [], [], []
    for k in range(kv_heads):
        by_slot = k < offloaded
        if 0 < k == offloaded:
            spec = pl.BlockSpec((16, HEAD_DIM), lambda i: (0, 0))
            few = small_call(
                copy_out, (1,), [spec], spec, jax.ShapeDtypeStruct((16, HEAD_DIM), bf16), [own_parts[0]], near[1][0]
            )
            sent = sent + [lax.all_gather(few, "node", axis=0)]
        dq, proj, own_part, *parts = attention(
            k, own[k][1], head_group, nodes, offloaded if by_slot else 0,
            owner_slot, query_rows, own[k][0], out_weight, pieces, near[k], old, sent,
        )
        old = [dq, proj] + (parts if k + 1 < offloaded else [])
        sent = [own_part]
        if by_slot:
            own_parts.append(own_part)
            if k + 1 == offloaded:
                came = lax.psum_scatter(parts[0], "node", scatter_dimension=0, tiled=False)
        else:
            sums.append(scatter_sum(*parts, own_part, nodes))
            sent = next(sums[-1])
            if k + 1 < kv_heads:
                sent = sums[-1].send(own_part)

    *earlier, last = sums
    early = [chain.send(own_part)[0] for chain in earlier] + [own_part]
    middle = last.send(own_part)[0]
    rows = proj.shape[0] // tp
    if tp == 2:
        me = lax.axis_index("tp").reshape(1)
        spec = (rows, COLUMNS)
        away = pl.pallas_call(
            lambda me, rows, after, out: copy_out(rows, after, out),
            grid_spec=pltpu.PrefetchScalarGridSpec(
                num_scalar_prefetch=1,
                grid=(proj.shape[1] // COLUMNS,),
                in_specs=[
                    pl.BlockSpec(spec, lambda j, me: (1 - me[0], j)),
                    pl.BlockSpec(memory_space=pl.ANY),
                ],
                out_specs=pl.BlockSpec(spec, lambda j, me: (0, j)),
            ),
            out_shape=jax.ShapeDtypeStruct((rows, proj.shape[1]), bf16),
            compiler_params=pltpu.CompilerParams(vmem_limit_bytes=63 * 1024 * 1024),
            cost_estimate=pl.CostEstimate(flops=2**10, bytes_accessed=2**12, transcendentals=0),
        )(me, proj, middle)
        here = lax.dynamic_slice_in_dim(proj, me[0] * rows, rows, 0)
        projected = here + lax.ppermute(away, "tp", [(0, 1), (1, 0)]).astype(f32)
        projected = projected.astype(bf16)
    else:
        projected = lax.psum_scatter(proj.astype(bf16), "tp", scatter_dimension=0, tiled=True)
    moved = last.send(early[0])[0]
    totals = []
    for chain in earlier + [last]:
        try:
            chain.send(moved)
        except StopIteration as end:
            totals.append(end.value)
    if offloaded:
        totals = [final_sum([own_parts[k], came[k]], moved) for k in range(offloaded)] + totals
    return (
        projected,
        dq,
        jnp.concatenate([total[:, :HEAD_DIM] for total in totals], axis=1),
        jnp.concatenate([total[:, HEAD_DIM:] for total in totals], axis=1),
    )


def solution(mesh):
    in_specs = (
        P("node", "tp"),
        P("node", "tp"),
        P("node", "tp"),
        P("tp", None),
        P(("node", "tp"), None),
        P(),
    )
    out_specs = (P(("node", "tp"), None), P("node", "tp"), P("node", "tp"), P("node", "tp"))
    return jax.shard_map(
        functools.partial(local, mesh.shape["tp"], mesh.shape["node"]),
        mesh=mesh, in_specs=in_specs, out_specs=out_specs, check_vma=False,
    )
```

```python
import functools

import jax
import jax.numpy as jnp
from jax import lax
from jax.experimental import pallas as pl
from jax.experimental.pallas import tpu as pltpu
from jax.sharding import PartitionSpec as P

HEAD_DIM = 128
NODE_LEN = 256
CHAIN = 8
LEAVES = 8
PAIR = 2 * HEAD_DIM
COLUMNS = 512

masked_score = -1e30
score_scale = HEAD_DIM ** (-0.5)
log2_e = 1.4426950408889634


def dot(a, b):
    return jnp.dot(a, b, preferred_element_type=jnp.float32)


def dot_nt(a, b):
    return lax.dot_general(a, b, (((1,), (1,)), ((), ())), preferred_element_type=jnp.float32)


def attend(layout, owner_slot, *refs):
    piece_count, near_count, after_count, chunk_head, by_slot, old_count, head = layout
    q_any, own_any, weight_any = refs[:3]
    pieces, refs = refs[3 : 3 + piece_count], refs[3 + piece_count :]
    near, refs = refs[:near_count], refs[near_count:]
    old, rest = refs[:old_count], refs[old_count + after_count :]
    dq_any, proj_any, own_any_grad = rest[:3]
    parts = rest[3 : 4 if by_slot else 5]
    (
        far_ref, own_ref, out_grad, weight, proj, att, s_ref, p_ref, qs, ups, q_t, up_t,
        m_ref, l_ref, acc_ref, own_grad, slots, far_sem, slot_sem, q_sem, piece_sem, sem,
    ) = rest[3 + len(parts) :]
    me = lax.axis_index("node")
    node_count = owner_slot.shape[0]
    tree_node = jnp.int32(0)
    for n in range(node_count):
        tree_node = jnp.where(owner_slot[n] == me, n, tree_node)
    tree_nodes = CHAIN + LEAVES
    first_node = tree_node // tree_nodes * tree_nodes
    depth = jnp.minimum(tree_node - first_node, CHAIN)
    lineage = [owner_slot[first_node + b] for b in range(CHAIN)]

    def ancestor(b):
        return lineage[b] if isinstance(b, int) else owner_slot[first_node + b]

    rows = qs.shape[0]
    heads = rows // NODE_LEN
    half = HEAD_DIM
    width = heads * HEAD_DIM
    factor = score_scale * log2_e
    stride = slots.shape[0] // 4

    def head_rows(h):
        return pl.ds(h * NODE_LEN, NODE_LEN)

    def head_columns(h, first=0):
        return pl.ds(first + h * HEAD_DIM, HEAD_DIM)

    q_copies = [
        pltpu.make_async_copy(
            q_any.at[:, head_columns(h, head * width)], qs.at[head_rows(h), :], q_sem.at[h]
        )
        for h in range(heads)
    ]
    def pair_copies(source, target, sems):
        return [
            pltpu.make_async_copy(
                source.at[:, pl.ds(i * source.shape[1] // 2 + chunk_head * half, half)],
                target.at[:, pl.ds(i * half, half)],
                sems[i],
            )
            for i in range(2)
        ]

    own_copies = pair_copies(own_any, own_ref, [sem.at[0], sem.at[2]])
    weight_copy = pltpu.make_async_copy(
        weight_any.at[pl.ds(head * width, width), :], weight, sem.at[1]
    )
    order = lax.axis_index("tp") if piece_count == 2 else 0
    piece_rows = pieces[0].shape[0]
    piece_copies = [
        pltpu.make_async_copy(
            piece,
            out_grad.at[pl.ds(pl.multiple_of((order ^ i) * piece_rows, piece_rows), piece_rows), :],
            piece_sem.at[i],
        )
        for i, piece in enumerate(pieces)
    ]
    for copy in own_copies + q_copies:
        copy.start()

    def far_copies(source, index, b):
        return pair_copies(
            source.at[index], far_ref.at[b], [far_sem.at[b], far_sem.at[CHAIN + b]]
        )

    def fetch(b, carry):
        if near_count == 1:
            for copy in far_copies(near[0], ancestor(b), b):
                copy.start()
            return carry
        away = ancestor(b) ^ me
        for kind in range(near_count):

            @pl.when(away % 4 == kind)
            def _():
                for copy in far_copies(near[kind], away // 4, b):
                    copy.start()

        return carry

    lax.fori_loop(0, depth, fetch, 0)

    def for_blocks(body):
        def two(i, carry):
            body(2 * i, carry)
            return body(2 * i + 1, carry)

        lax.fori_loop(0, depth // 2, two, 0)

        @pl.when(depth % 2 == 1)
        def _():
            body(depth - 1, 0)

    def fold_max(s):
        return jnp.maximum(s[:, :half], s[:, half:])

    for copy in own_copies + q_copies:
        copy.wait()
    s = dot_nt(qs[...], own_ref[:, :half])
    row = lax.broadcasted_iota(jnp.int32, (rows, NODE_LEN), 0) % NODE_LEN
    col = lax.broadcasted_iota(jnp.int32, (rows, NODE_LEN), 1)
    s = jnp.where(col <= row, s, masked_score)
    s_ref[CHAIN] = s
    m_ref[...] = fold_max(s)

    def score_block(b, carry):
        for copy in far_copies(near[0], 0, b):
            copy.wait()
        s = dot_nt(qs[...], far_ref[b, :, :half])
        s_ref[b] = s
        m_ref[...] = jnp.maximum(m_ref[...], fold_max(s))
        return carry

    for_blocks(score_block)

    late_copies = [weight_copy] + piece_copies
    if head > 0:
        late_copies.append(pltpu.make_async_copy(old[1], proj, sem.at[3]))
    for copy in late_copies:
        copy.start()
    m_ref[...] = jnp.broadcast_to(jnp.max(m_ref[...], axis=1, keepdims=True), (rows, half))

    def weigh(b, values):
        top = m_ref[...]
        s = s_ref[b]
        p_low = jnp.exp2((s[:, :half] - top) * factor)
        p_high = jnp.exp2((s[:, half:] - top) * factor)
        p = jnp.concatenate([p_low, p_high], axis=1).astype(jnp.bfloat16)
        p_ref[b] = p
        return p_low + p_high, dot(p, values)

    part_sum, part = weigh(CHAIN, own_ref[:, half:])
    l_ref[...] = part_sum
    acc_ref[...] = part

    def forward_block(b, carry):
        part_sum, part = weigh(b, far_ref[b, :, half:])
        l_ref[...] += part_sum
        acc_ref[...] += part
        return carry

    for_blocks(forward_block)
    inverse = 1.0 / jnp.broadcast_to(jnp.sum(l_ref[...], axis=1, keepdims=True), (rows, half))
    l_ref[...] = inverse
    attended = (acc_ref[...] * inverse).astype(jnp.bfloat16)
    for h in range(heads):
        att[:, head_columns(h)] = attended[h * NODE_LEN : (h + 1) * NODE_LEN, :]

    for copy in late_copies:
        copy.wait()
    for h in range(0, heads, 2):
        count = min(2, heads - h)
        two = dot_nt(out_grad[...], weight[h * HEAD_DIM : (h + count) * HEAD_DIM, :])
        for i in range(count):
            ups[head_rows(h + i), :] = two[:, i * HEAD_DIM : (i + 1) * HEAD_DIM].astype(jnp.bfloat16)

    def project(n, carry):
        columns = pl.ds(pl.multiple_of(n * COLUMNS, COLUMNS), COLUMNS)
        share = dot(att[...], weight[:, columns])
        proj[:, columns] = share if head == 0 else proj[:, columns] + share
        return carry

    lax.fori_loop(0, weight.shape[1] // COLUMNS, project, 0)
    proj_out = pltpu.make_async_copy(proj, proj_any, sem.at[4])
    proj_out.start()

    upstream = ups[...].astype(jnp.float32)
    corr_ref = m_ref
    corr_ref[...] = jnp.broadcast_to(
        jnp.sum(upstream * attended.astype(jnp.float32), axis=1, keepdims=True), (rows, half)
    )
    q_t[...] = (qs[...].astype(jnp.float32) * (inverse * score_scale)).astype(jnp.bfloat16).T
    up_t[...] = (upstream * inverse).astype(jnp.bfloat16).T

    def backward(b, keys, values):
        corr = corr_ref[...]
        p = p_ref[b]
        d_prob = dot_nt(ups[...], values)
        centred = jnp.concatenate([d_prob[:, :half] - corr, d_prob[:, half:] - corr], axis=1)
        d_score = (p.astype(jnp.float32) * centred).astype(jnp.bfloat16)
        grad = jnp.concatenate([dot(q_t[...], d_score), dot(up_t[...], p)], axis=0)
        return dot(d_score, keys), grad

    def slot_place(b):
        if by_slot:
            return ancestor(b)
        away = ancestor(b) ^ me
        kind = away % 4
        return away // 4 + stride * jnp.where(kind == 0, 0, jnp.where(kind == 2, 1, 2 + kind // 2))

    def slot_copy(slot, target):
        return pltpu.make_async_copy(slots.at[slot], target, slot_sem.at[slot])

    def send_out(slot):
        if by_slot:
            slot_copy(slot, parts[0].at[slot, head]).start()
            return

        @pl.when(slot < 2 * stride)
        def _():
            slot_copy(slot, parts[0].at[slot]).start()

        @pl.when(slot >= 2 * stride)
        def _():
            slot_copy(slot, parts[1].at[slot - 2 * stride]).start()

    def is_far(slot):
        return functools.reduce(
            jnp.logical_or, [jnp.logical_and(b < depth, slot_place(b) == slot) for b in range(CHAIN)]
        )

    def clear(slot, carry):
        @pl.when(jnp.logical_not(is_far(slot)))
        def _():
            slots[slot] = jnp.zeros(slots.shape[1:], slots.dtype)
            send_out(slot)

        return carry

    lax.fori_loop(0, slots.shape[0], clear, 0)
    part, grad = backward(CHAIN, own_ref[:, :half], own_ref[:, half:])
    acc_ref[...] = part
    own_grad[...] = grad.T
    own_out = pltpu.make_async_copy(own_grad, own_any_grad, sem.at[3])
    own_out.start()

    def backward_block(b, carry):
        part, grad = backward(b, far_ref[b, :, :half], far_ref[b, :, half:])
        acc_ref[...] += part
        block = grad.astype(jnp.bfloat16).T
        slot = slot_place(b)
        slots[slot] = block
        send_out(slot)
        return carry

    for_blocks(backward_block)
    query_grad = (acc_ref[...] * (l_ref[...] * score_scale)).astype(jnp.bfloat16)
    for h in range(heads):
        att[:, head_columns(h)] = query_grad[h * NODE_LEN : (h + 1) * NODE_LEN, :]
    dq_out = pltpu.make_async_copy(att, dq_any.at[:, pl.ds(head * width, width)], sem.at[5])
    dq_out.start()
    own_out.wait()

    def finish(slot, carry):
        slot_copy(slot, parts[0].at[0, head] if by_slot else parts[0].at[0]).wait()
        return carry

    lax.fori_loop(0, slots.shape[0], finish, 0)
    proj_out.wait()
    dq_out.wait()


def attention(
    head, chunk_head, head_group, nodes, slot_heads,
    owner_slot, query_rows, own, weight, pieces, near, old, after,
):
    bf16, f32 = jnp.bfloat16, jnp.float32
    stride = nodes // 4
    width = head_group * HEAD_DIM
    rows = head_group * NODE_LEN
    d_out = weight.shape[1]
    block = (NODE_LEN, PAIR)
    anywhere = pl.BlockSpec(memory_space=pl.ANY)
    in_smem = pl.BlockSpec(memory_space=pltpu.SMEM)
    if slot_heads:
        parts = [jax.ShapeDtypeStruct((nodes, slot_heads) + block, bf16)]
    else:
        parts = [jax.ShapeDtypeStruct((2 * stride,) + block, bf16)] * 2
    first_old = 4 + len(pieces) + len(near)
    aliases = {first_old + i: i if i < 2 else 3 for i in range(len(old))}
    layout = (len(pieces), len(near), len(after), chunk_head, bool(slot_heads), len(old), head)
    blocks = (CHAIN + 1) * head_group
    return pl.pallas_call(
        functools.partial(attend, layout),
        in_specs=[in_smem] + [anywhere] * (3 + len(pieces) + len(near) + len(old) + len(after)),
        out_specs=[anywhere] * (3 + len(parts)),
        out_shape=[
            jax.ShapeDtypeStruct(query_rows.shape, bf16),
            jax.ShapeDtypeStruct((NODE_LEN, d_out), f32),
            jax.ShapeDtypeStruct(block, f32),
        ]
        + parts,
        input_output_aliases=aliases,
        scratch_shapes=[
            pltpu.VMEM((CHAIN,) + block, bf16),
            pltpu.VMEM(block, bf16),
            pltpu.VMEM((NODE_LEN, d_out), bf16),
            pltpu.VMEM((width, d_out), bf16),
            pltpu.VMEM((NODE_LEN, d_out), f32),
            pltpu.VMEM((NODE_LEN, width), bf16),
            pltpu.VMEM((CHAIN + 1, rows, NODE_LEN), f32),
            pltpu.VMEM((CHAIN + 1, rows, NODE_LEN), bf16),
            pltpu.VMEM((rows, HEAD_DIM), bf16),
            pltpu.VMEM((rows, HEAD_DIM), bf16),
            pltpu.VMEM((HEAD_DIM, rows), bf16),
            pltpu.VMEM((HEAD_DIM, rows), bf16),
            pltpu.VMEM((rows, HEAD_DIM), f32),
            pltpu.VMEM((rows, HEAD_DIM), f32),
            pltpu.VMEM((rows, HEAD_DIM), f32),
            pltpu.VMEM(block, f32),
            pltpu.VMEM((nodes,) + block, bf16),
            pltpu.SemaphoreType.DMA((2 * CHAIN,)),
            pltpu.SemaphoreType.DMA((nodes,)),
            pltpu.SemaphoreType.DMA((head_group,)),
            pltpu.SemaphoreType.DMA((2,)),
            pltpu.SemaphoreType.DMA((6,)),
        ],
        compiler_params=pltpu.CompilerParams(vmem_limit_bytes=63 * 1024 * 1024),
        cost_estimate=pl.CostEstimate(
            flops=2 * blocks * NODE_LEN,
            bytes_accessed=2**20,
            transcendentals=0,
        ),
    )(owner_slot, query_rows, own, weight, *pieces, *near, *old, *after)


def swap(block, mask, nodes):
    return lax.ppermute(block, "node", [(i, i ^ mask) for i in range(nodes)])


def gather_near(own, nodes):
    stride = nodes // 4
    line = jnp.stack([own] + [swap(own, 4 * d, nodes) for d in range(1, stride)])
    cross = swap(line, 2, nodes)
    return [line, swap(line, 1, nodes), cross, swap(cross, 1, nodes)]


def add_level_1(keep, cross, came_keep, came_cross, after, cross_sum, keep_sum):
    f32 = jnp.float32
    cross_sum[...] = (cross[...].astype(f32) + came_cross[...].astype(f32)).astype(jnp.bfloat16)
    keep_sum[...] = keep[...].astype(f32) + came_keep[...].astype(f32)


def add_level_2(keep, came, *refs):
    keep_sum, *sent = refs[1:]
    total = keep[0] + came[0].astype(jnp.float32)
    for d in range(len(sent) + 1):

        @pl.when(pl.program_id(0) == d)
        def _():
            if d == 0:
                keep_sum[...] = total
            else:
                sent[d - 1][...] = total.astype(jnp.bfloat16)


def add_all(*refs):
    *parts, after, total = refs
    total[...] = functools.reduce(jnp.add, [part[...].astype(jnp.float32) for part in parts]).astype(total.dtype)


def small_call(kernel, grid, in_specs, out_specs, out_shape, operands, after):
    return pl.pallas_call(
        kernel,
        grid=grid,
        in_specs=in_specs + [pl.BlockSpec(memory_space=pl.ANY)],
        out_specs=out_specs,
        out_shape=out_shape,
        compiler_params=pltpu.CompilerParams(vmem_limit_bytes=16 * 1024 * 1024),
        cost_estimate=pl.CostEstimate(flops=2**10, bytes_accessed=2**12, transcendentals=0),
    )(*operands, after)


def scatter_sum(kept, away, own_part, nodes):
    bf16, f32 = jnp.bfloat16, jnp.float32
    stride = nodes // 4
    came = swap(away, 1, nodes)
    after = yield [away]
    block = kept.shape[1:]
    one = pl.BlockSpec((1,) + block, lambda d: (d, 0, 0))
    far = pl.BlockSpec((1,) + block, lambda d: (stride + d, 0, 0))
    whole = pl.BlockSpec(block, lambda d: (0, 0))
    cross, keep = small_call(
        add_level_1,
        (stride,),
        [one, far, one, far],
        [one, one],
        [jax.ShapeDtypeStruct((stride,) + block, t) for t in (bf16, f32)],
        [kept, kept, came, came],
        after,
    )
    came = swap(cross, 2, nodes)
    after = yield [cross]
    keep, *sent = small_call(
        add_level_2,
        (stride,),
        [one, one],
        [whole] * stride,
        [jax.ShapeDtypeStruct(block, f32)] + [jax.ShapeDtypeStruct(block, bf16)] * (stride - 1),
        [keep, came],
        after,
    )
    came = [swap(part, 4 * (d + 1), nodes) for d, part in enumerate(sent)]
    after = yield sent
    parts = [own_part, keep] + came
    return small_call(
        add_all, (1,), [whole] * len(parts), whole, jax.ShapeDtypeStruct(block, bf16), parts, after
    )


def local(tp, nodes, query_rows, key_rows, value_rows, out_weight, out_grad, owner_slot):
    bf16, f32 = jnp.bfloat16, jnp.float32
    kv_width = key_rows.shape[1]
    kv_heads = kv_width // HEAD_DIM
    head_group = query_rows.shape[1] // kv_width
    if tp == 2:
        pieces = [out_grad, lax.ppermute(out_grad, "tp", [(0, 1), (1, 0)])]
    else:
        pieces = [lax.all_gather(out_grad, "tp", axis=0, tiled=True)]

    own, near = {}, {}
    for first, heads in [(0, 1)] + ([(1, kv_heads - 1)] if kv_heads > 1 else []):
        columns = slice(first * HEAD_DIM, (first + heads) * HEAD_DIM)
        packed = jnp.concatenate([key_rows[:, columns], value_rows[:, columns]], axis=1)
        if first == 0:
            blocks = gather_near(packed, nodes)
        else:
            blocks = [lax.all_gather(packed, "node", axis=0, tiled=False)]
        for i in range(heads):
            own[first + i], near[first + i] = (packed, i), blocks

    offloaded = max(0, kv_heads - 2)
    old, sums, own_parts, sent = [], [], [], []
    for k in range(kv_heads):
        by_slot = k < offloaded
        dq, proj, own_part, *parts = attention(
            k, own[k][1], head_group, nodes, offloaded if by_slot else 0,
            owner_slot, query_rows, own[k][0], out_weight, pieces, near[k], old, sent,
        )
        old = [dq, proj] + (parts if k + 1 < offloaded else [])
        sent = [own_part]
        if by_slot:
            own_parts.append(own_part)
            if k + 1 == offloaded:
                came = lax.psum_scatter(parts[0], "node", scatter_dimension=0, tiled=False)
        else:
            sums.append(scatter_sum(*parts, own_part, nodes))
            sent = next(sums[-1])
            if k + 1 < kv_heads:
                sent = sums[-1].send(own_part)

    *earlier, last = sums
    middle = last.send(own_part)[0]
    early = [chain.send(middle)[0] for chain in earlier] + [own_part]
    rows = proj.shape[0] // tp
    if tp == 2:
        me = lax.axis_index("tp")
        away = lax.dynamic_slice_in_dim(proj, (1 - me) * rows, rows, 0).astype(bf16)
        here = lax.dynamic_slice_in_dim(proj, me * rows, rows, 0)
        projected = here + lax.ppermute(away, "tp", [(0, 1), (1, 0)]).astype(f32)
        projected = projected.astype(bf16)
    else:
        projected = lax.psum_scatter(proj.astype(bf16), "tp", scatter_dimension=0, tiled=True)
    moved = last.send(early[0])[0]
    totals = []
    for chain in earlier + [last]:
        try:
            chain.send(moved)
        except StopIteration as end:
            totals.append(end.value)
    if offloaded:
        totals = [(own_parts[k] + came[k].astype(f32)).astype(bf16) for k in range(offloaded)] + totals
    return (
        projected,
        dq,
        jnp.concatenate([total[:, :HEAD_DIM] for total in totals], axis=1),
        jnp.concatenate([total[:, HEAD_DIM:] for total in totals], axis=1),
    )


def solution(mesh):
    in_specs = (
        P("node", "tp"),
        P("node", "tp"),
        P("node", "tp"),
        P("tp", None),
        P(("node", "tp"), None),
        P(),
    )
    out_specs = (P(("node", "tp"), None), P("node", "tp"), P("node", "tp"), P("node", "tp"))
    return jax.shard_map(
        functools.partial(local, mesh.shape["tp"], mesh.shape["node"]),
        mesh=mesh, in_specs=in_specs, out_specs=out_specs, check_vma=False,
    )
```

```python
import functools

import jax
import jax.numpy as jnp
from jax import lax
from jax.experimental import pallas as pl
from jax.experimental.pallas import tpu as pltpu
from jax.sharding import PartitionSpec as P

HEAD_DIM = 128
NODE_LEN = 256
CHAIN = 8
LEAVES = 8
PAIR = 2 * HEAD_DIM
COLUMNS = 512

masked_score = -1e30
score_scale = HEAD_DIM ** (-0.5)
log2_e = 1.4426950408889634


def dot(a, b):
    return jnp.dot(a, b, preferred_element_type=jnp.float32)


def dot_nt(a, b):
    return lax.dot_general(a, b, (((1,), (1,)), ((), ())), preferred_element_type=jnp.float32)


def attend(layout, owner_slot, *refs):
    piece_count, near_count, after_count, chunk_head, by_slot, old_count, head = layout
    q_any, own_any, weight_any = refs[:3]
    pieces, refs = refs[3 : 3 + piece_count], refs[3 + piece_count :]
    near, refs = refs[:near_count], refs[near_count:]
    old, rest = refs[:old_count], refs[old_count + after_count :]
    dq_any, proj_any, own_any_grad = rest[:3]
    parts = rest[3 : 4 if by_slot else 5]
    (
        far_ref, own_ref, out_grad, weight, proj, att, s_ref, p_ref, qs, ups, q_t, up_t,
        m_ref, l_ref, acc_ref, own_grad, slots, far_sem, slot_sem, q_sem, piece_sem, sem,
    ) = rest[3 + len(parts) :]
    me = lax.axis_index("node")
    node_count = owner_slot.shape[0]
    tree_node = jnp.int32(0)
    for n in range(node_count):
        tree_node = jnp.where(owner_slot[n] == me, n, tree_node)
    tree_nodes = CHAIN + LEAVES
    first_node = tree_node // tree_nodes * tree_nodes
    depth = jnp.minimum(tree_node - first_node, CHAIN)
    lineage = [owner_slot[first_node + b] for b in range(CHAIN)]

    def ancestor(b):
        return lineage[b] if isinstance(b, int) else owner_slot[first_node + b]

    rows = qs.shape[0]
    heads = rows // NODE_LEN
    half = HEAD_DIM
    width = heads * HEAD_DIM
    factor = score_scale * log2_e
    stride = slots.shape[0] // 4

    def head_rows(h):
        return pl.ds(h * NODE_LEN, NODE_LEN)

    def head_columns(h, first=0):
        return pl.ds(first + h * HEAD_DIM, HEAD_DIM)

    q_copies = [
        pltpu.make_async_copy(
            q_any.at[:, head_columns(h, head * width)], qs.at[head_rows(h), :], q_sem.at[h]
        )
        for h in range(heads)
    ]
    def pair_copies(source, target, sems):
        return [
            pltpu.make_async_copy(
                source.at[:, pl.ds(i * source.shape[1] // 2 + chunk_head * half, half)],
                target.at[:, pl.ds(i * half, half)],
                sems[i],
            )
            for i in range(2)
        ]

    own_copies = pair_copies(own_any, own_ref, [sem.at[0], sem.at[2]])
    weight_copy = pltpu.make_async_copy(
        weight_any.at[pl.ds(head * width, width), :], weight, sem.at[1]
    )
    order = lax.axis_index("tp") if piece_count == 2 else 0
    piece_rows = pieces[0].shape[0]
    piece_copies = [
        pltpu.make_async_copy(
            piece,
            out_grad.at[pl.ds(pl.multiple_of((order ^ i) * piece_rows, piece_rows), piece_rows), :],
            piece_sem.at[i],
        )
        for i, piece in enumerate(pieces)
    ]
    for copy in own_copies + q_copies:
        copy.start()

    def far_copies(source, index, b):
        return pair_copies(
            source.at[index], far_ref.at[b], [far_sem.at[b], far_sem.at[CHAIN + b]]
        )

    def fetch(b, carry):
        if near_count == 1:
            for copy in far_copies(near[0], ancestor(b), b):
                copy.start()
            return carry
        away = ancestor(b) ^ me
        for kind in range(near_count):

            @pl.when(away % 4 == kind)
            def _():
                for copy in far_copies(near[kind], away // 4, b):
                    copy.start()

        return carry

    lax.fori_loop(0, depth, fetch, 0)

    late_copies = [weight_copy] + piece_copies
    if head > 0:
        late_copies.append(pltpu.make_async_copy(old[1], proj, sem.at[3]))
    for copy in late_copies:
        copy.start()

    def fold_max(s):
        return jnp.maximum(s[:, :half], s[:, half:])

    for copy in own_copies + q_copies:
        copy.wait()
    s = dot_nt(qs[...], own_ref[:, :half])
    row = lax.broadcasted_iota(jnp.int32, (rows, NODE_LEN), 0) % NODE_LEN
    col = lax.broadcasted_iota(jnp.int32, (rows, NODE_LEN), 1)
    s = jnp.where(col <= row, s, masked_score)
    s_ref[CHAIN] = s
    m_ref[...] = fold_max(s)

    def score_block(b, carry):
        for copy in far_copies(near[0], 0, b):
            copy.wait()
        s = dot_nt(qs[...], far_ref[b, :, :half])
        s_ref[b] = s
        m_ref[...] = jnp.maximum(m_ref[...], fold_max(s))
        return carry

    lax.fori_loop(0, depth, score_block, 0)
    m_ref[...] = jnp.broadcast_to(jnp.max(m_ref[...], axis=1, keepdims=True), (rows, half))

    def weigh(b, values):
        top = m_ref[...]
        s = s_ref[b]
        p_low = jnp.exp2((s[:, :half] - top) * factor)
        p_high = jnp.exp2((s[:, half:] - top) * factor)
        p = jnp.concatenate([p_low, p_high], axis=1).astype(jnp.bfloat16)
        p_ref[b] = p
        return p_low + p_high, dot(p, values)

    part_sum, part = weigh(CHAIN, own_ref[:, half:])
    l_ref[...] = part_sum
    acc_ref[...] = part

    def forward_block(b, carry):
        part_sum, part = weigh(b, far_ref[b, :, half:])
        l_ref[...] += part_sum
        acc_ref[...] += part
        return carry

    lax.fori_loop(0, depth, forward_block, 0)
    inverse = 1.0 / jnp.broadcast_to(jnp.sum(l_ref[...], axis=1, keepdims=True), (rows, half))
    l_ref[...] = inverse
    attended = (acc_ref[...] * inverse).astype(jnp.bfloat16)
    for h in range(heads):
        att[:, head_columns(h)] = attended[h * NODE_LEN : (h + 1) * NODE_LEN, :]

    for copy in late_copies:
        copy.wait()
    for h in range(0, heads, 2):
        count = min(2, heads - h)
        two = dot_nt(out_grad[...], weight[h * HEAD_DIM : (h + count) * HEAD_DIM, :])
        for i in range(count):
            ups[head_rows(h + i), :] = two[:, i * HEAD_DIM : (i + 1) * HEAD_DIM].astype(jnp.bfloat16)

    def project(n, carry):
        columns = pl.ds(pl.multiple_of(n * COLUMNS, COLUMNS), COLUMNS)
        share = dot(att[...], weight[:, columns])
        proj[:, columns] = share if head == 0 else proj[:, columns] + share
        return carry

    lax.fori_loop(0, weight.shape[1] // COLUMNS, project, 0)
    proj_out = pltpu.make_async_copy(proj, proj_any, sem.at[4])
    proj_out.start()

    upstream = ups[...].astype(jnp.float32)
    corr_ref = m_ref
    corr_ref[...] = jnp.broadcast_to(
        jnp.sum(upstream * attended.astype(jnp.float32), axis=1, keepdims=True), (rows, half)
    )
    q_t[...] = (qs[...].astype(jnp.float32) * (inverse * score_scale)).astype(jnp.bfloat16).T
    up_t[...] = (upstream * inverse).astype(jnp.bfloat16).T

    def backward(b, keys, values):
        corr = corr_ref[...]
        p = p_ref[b]
        d_prob = dot_nt(ups[...], values)
        centred = jnp.concatenate([d_prob[:, :half] - corr, d_prob[:, half:] - corr], axis=1)
        d_score = (p.astype(jnp.float32) * centred).astype(jnp.bfloat16)
        grad = jnp.concatenate([dot(q_t[...], d_score), dot(up_t[...], p)], axis=0)
        return dot(d_score, keys), grad

    def slot_place(b):
        if by_slot:
            return ancestor(b)
        away = ancestor(b) ^ me
        kind = away % 4
        return away // 4 + stride * jnp.where(kind == 0, 0, jnp.where(kind == 2, 1, 2 + kind // 2))

    slots[...] = jnp.zeros_like(slots)
    part, grad = backward(CHAIN, own_ref[:, :half], own_ref[:, half:])
    acc_ref[...] = part
    own_grad[...] = grad.T
    own_out = pltpu.make_async_copy(own_grad, own_any_grad, sem.at[3])
    own_out.start()

    def backward_block(b, carry):
        part, grad = backward(b, far_ref[b, :, :half], far_ref[b, :, half:])
        acc_ref[...] += part
        block = grad.astype(jnp.bfloat16).T
        slots[slot_place(b)] = block
        return carry

    lax.fori_loop(0, depth, backward_block, 0)
    if by_slot:
        part_copies = [pltpu.make_async_copy(slots, parts[0].at[:, head], slot_sem.at[0])]
    else:
        part_copies = [
            pltpu.make_async_copy(slots.at[pl.ds(2 * stride * i, 2 * stride)], part, slot_sem.at[i])
            for i, part in enumerate(parts)
        ]
    for copy in part_copies:
        copy.start()
    query_grad = (acc_ref[...] * (l_ref[...] * score_scale)).astype(jnp.bfloat16)
    for h in range(heads):
        att[:, head_columns(h)] = query_grad[h * NODE_LEN : (h + 1) * NODE_LEN, :]
    dq_out = pltpu.make_async_copy(att, dq_any.at[:, pl.ds(head * width, width)], sem.at[5])
    dq_out.start()
    for copy in part_copies + [own_out]:
        copy.wait()
    proj_out.wait()
    dq_out.wait()


def attention(
    head, chunk_head, head_group, nodes, slot_heads,
    owner_slot, query_rows, own, weight, pieces, near, old, after,
):
    bf16, f32 = jnp.bfloat16, jnp.float32
    stride = nodes // 4
    width = head_group * HEAD_DIM
    rows = head_group * NODE_LEN
    d_out = weight.shape[1]
    block = (NODE_LEN, PAIR)
    anywhere = pl.BlockSpec(memory_space=pl.ANY)
    in_smem = pl.BlockSpec(memory_space=pltpu.SMEM)
    if slot_heads:
        parts = [jax.ShapeDtypeStruct((nodes, slot_heads) + block, bf16)]
    else:
        parts = [jax.ShapeDtypeStruct((2 * stride,) + block, bf16)] * 2
    first_old = 4 + len(pieces) + len(near)
    aliases = {first_old + i: i if i < 2 else 3 for i in range(len(old))}
    layout = (len(pieces), len(near), len(after), chunk_head, bool(slot_heads), len(old), head)
    blocks = (CHAIN + 1) * head_group
    return pl.pallas_call(
        functools.partial(attend, layout),
        in_specs=[in_smem] + [anywhere] * (3 + len(pieces) + len(near) + len(old) + len(after)),
        out_specs=[anywhere] * (3 + len(parts)),
        out_shape=[
            jax.ShapeDtypeStruct(query_rows.shape, bf16),
            jax.ShapeDtypeStruct((NODE_LEN, d_out), f32),
            jax.ShapeDtypeStruct(block, f32),
        ]
        + parts,
        input_output_aliases=aliases,
        scratch_shapes=[
            pltpu.VMEM((CHAIN,) + block, bf16),
            pltpu.VMEM(block, bf16),
            pltpu.VMEM((NODE_LEN, d_out), bf16),
            pltpu.VMEM((width, d_out), bf16),
            pltpu.VMEM((NODE_LEN, d_out), f32),
            pltpu.VMEM((NODE_LEN, width), bf16),
            pltpu.VMEM((CHAIN + 1, rows, NODE_LEN), f32),
            pltpu.VMEM((CHAIN + 1, rows, NODE_LEN), bf16),
            pltpu.VMEM((rows, HEAD_DIM), bf16),
            pltpu.VMEM((rows, HEAD_DIM), bf16),
            pltpu.VMEM((HEAD_DIM, rows), bf16),
            pltpu.VMEM((HEAD_DIM, rows), bf16),
            pltpu.VMEM((rows, HEAD_DIM), f32),
            pltpu.VMEM((rows, HEAD_DIM), f32),
            pltpu.VMEM((rows, HEAD_DIM), f32),
            pltpu.VMEM(block, f32),
            pltpu.VMEM((nodes,) + block, bf16),
            pltpu.SemaphoreType.DMA((2 * CHAIN,)),
            pltpu.SemaphoreType.DMA((2,)),
            pltpu.SemaphoreType.DMA((head_group,)),
            pltpu.SemaphoreType.DMA((2,)),
            pltpu.SemaphoreType.DMA((6,)),
        ],
        compiler_params=pltpu.CompilerParams(vmem_limit_bytes=63 * 1024 * 1024),
        cost_estimate=pl.CostEstimate(
            flops=2 * blocks * NODE_LEN,
            bytes_accessed=2**20,
            transcendentals=0,
        ),
    )(owner_slot, query_rows, own, weight, *pieces, *near, *old, *after)


def zero_of(value):
    return jnp.minimum(jnp.abs(value.reshape(-1)[0].astype(jnp.float32)), 0.0)


def swap(block, mask, nodes):
    return lax.ppermute(block, "node", [(i, i ^ mask) for i in range(nodes)])


def gather_near(own, nodes):
    stride = nodes // 4
    line = jnp.stack([own] + [swap(own, 4 * d, nodes) for d in range(1, stride)])
    cross = swap(line, 2, nodes)
    return [line, swap(line, 1, nodes), cross, swap(cross, 1, nodes)]


def add_level_1(keep, cross, came_keep, came_cross, after, cross_sum, keep_sum):
    f32 = jnp.float32
    cross_sum[...] = (cross[...].astype(f32) + came_cross[...].astype(f32)).astype(jnp.bfloat16)
    keep_sum[...] = keep[...].astype(f32) + came_keep[...].astype(f32)


def add_level_2(keep, came, *refs):
    keep_sum, *sent = refs[1:]
    total = keep[0] + came[0].astype(jnp.float32)
    for d in range(len(sent) + 1):

        @pl.when(pl.program_id(0) == d)
        def _():
            if d == 0:
                keep_sum[...] = total
            else:
                sent[d - 1][...] = total.astype(jnp.bfloat16)


def add_all(*refs):
    *parts, after, total = refs
    total[...] = functools.reduce(jnp.add, [part[...].astype(jnp.float32) for part in parts]).astype(total.dtype)


def small_call(kernel, grid, in_specs, out_specs, out_shape, operands, after):
    return pl.pallas_call(
        kernel,
        grid=grid,
        in_specs=in_specs + [pl.BlockSpec(memory_space=pl.ANY)],
        out_specs=out_specs,
        out_shape=out_shape,
        compiler_params=pltpu.CompilerParams(vmem_limit_bytes=16 * 1024 * 1024),
        cost_estimate=pl.CostEstimate(flops=2**10, bytes_accessed=2**12, transcendentals=0),
    )(*operands, after)


def scatter_sum(kept, away, own_part, nodes):
    bf16, f32 = jnp.bfloat16, jnp.float32
    stride = nodes // 4
    came = swap(away, 1, nodes)
    after = yield [away]
    block = kept.shape[1:]
    one = pl.BlockSpec((1,) + block, lambda d: (d, 0, 0))
    far = pl.BlockSpec((1,) + block, lambda d: (stride + d, 0, 0))
    whole = pl.BlockSpec(block, lambda d: (0, 0))
    cross, keep = small_call(
        add_level_1,
        (stride,),
        [one, far, one, far],
        [one, one],
        [jax.ShapeDtypeStruct((stride,) + block, t) for t in (bf16, f32)],
        [kept, kept, came, came],
        after,
    )
    came = swap(cross, 2, nodes)
    after = yield [cross]
    keep, *sent = small_call(
        add_level_2,
        (stride,),
        [one, one],
        [whole] * stride,
        [jax.ShapeDtypeStruct(block, f32)] + [jax.ShapeDtypeStruct(block, bf16)] * (stride - 1),
        [keep, came],
        after,
    )
    came = [swap(part, 4 * (d + 1), nodes) for d, part in enumerate(sent)]
    after = yield sent
    parts = [own_part, keep] + came
    return small_call(
        add_all, (1,), [whole] * len(parts), whole, jax.ShapeDtypeStruct(block, bf16), parts, after
    )


def local(tp, nodes, query_rows, key_rows, value_rows, out_weight, out_grad, owner_slot):
    bf16, f32 = jnp.bfloat16, jnp.float32
    kv_width = key_rows.shape[1]
    kv_heads = kv_width // HEAD_DIM
    head_group = query_rows.shape[1] // kv_width
    if tp == 2:
        pieces = [out_grad, lax.ppermute(out_grad, "tp", [(0, 1), (1, 0)])]
    else:
        pieces = [lax.all_gather(out_grad, "tp", axis=0, tiled=True)]

    own, near = {}, {}
    for first, heads in [(0, 1)] + ([(1, kv_heads - 1)] if kv_heads > 1 else []):
        columns = slice(first * HEAD_DIM, (first + heads) * HEAD_DIM)
        packed = jnp.concatenate([key_rows[:, columns], value_rows[:, columns]], axis=1)
        if first == 0:
            blocks = gather_near(packed, nodes)
        else:
            blocks = [lax.all_gather(packed, "node", axis=0, tiled=False)]
        for i in range(heads):
            own[first + i], near[first + i] = (packed, i), blocks

    offloaded = max(0, kv_heads - 2)
    old, sums, own_parts, sent = [], [], [], []
    for k in range(kv_heads):
        by_slot = k < offloaded
        dq, proj, own_part, *parts = attention(
            k, own[k][1], head_group, nodes, offloaded if by_slot else 0,
            owner_slot, query_rows, own[k][0], out_weight, pieces, near[k], old, sent,
        )
        old = [dq, proj] + (parts if k + 1 < offloaded else [])
        sent = [own_part]
        if by_slot:
            own_parts.append(own_part)
            if k + 1 == offloaded:
                came = lax.psum_scatter(parts[0], "node", scatter_dimension=0, tiled=False)
        else:
            sums.append(scatter_sum(*parts, own_part, nodes))
            sent = next(sums[-1])
            if k + 1 < kv_heads:
                sent = sums[-1].send(own_part)

    *earlier, last = sums
    early = [chain.send(own_part)[0] for chain in earlier] + [own_part]
    middle = last.send(early[0])[0]
    rows = proj.shape[0] // tp
    if tp == 2:
        me = lax.axis_index("tp")
        away = lax.dynamic_slice_in_dim(proj, (1 - me) * rows, rows, 0)
        away = (away + zero_of(early[0])).astype(bf16)
        here = lax.dynamic_slice_in_dim(proj, me * rows, rows, 0)
        projected = here + lax.ppermute(away, "tp", [(0, 1), (1, 0)]).astype(f32)
        projected = projected.astype(bf16)
    else:
        projected = lax.psum_scatter(proj.astype(bf16), "tp", scatter_dimension=0, tiled=True)
    moved = last.send(middle)[0]
    totals = []
    for chain in earlier + [last]:
        try:
            chain.send(moved)
        except StopIteration as end:
            totals.append(end.value)
    if offloaded:
        totals = [(own_parts[k] + came[k].astype(f32)).astype(bf16) for k in range(offloaded)] + totals
    return (
        projected,
        dq,
        jnp.concatenate([total[:, :HEAD_DIM] for total in totals], axis=1),
        jnp.concatenate([total[:, HEAD_DIM:] for total in totals], axis=1),
    )


def solution(mesh):
    in_specs = (
        P("node", "tp"),
        P("node", "tp"),
        P("node", "tp"),
        P("tp", None),
        P(("node", "tp"), None),
        P(),
    )
    out_specs = (P(("node", "tp"), None), P("node", "tp"), P("node", "tp"), P("node", "tp"))
    return jax.shard_map(
        functools.partial(local, mesh.shape["tp"], mesh.shape["node"]),
        mesh=mesh, in_specs=in_specs, out_specs=out_specs, check_vma=False,
    )
```

```python
import functools

import jax
import jax.numpy as jnp
from jax import lax
from jax.experimental import pallas as pl
from jax.experimental.pallas import tpu as pltpu
from jax.sharding import PartitionSpec as P

HEAD_DIM = 128
NODE_LEN = 256
CHAIN = 8
LEAVES = 8
PAIR = 2 * HEAD_DIM
COLUMNS = 512

masked_score = -1e30
score_scale = HEAD_DIM ** (-0.5)
log2_e = 1.4426950408889634


def dot(a, b):
    return jnp.dot(a, b, preferred_element_type=jnp.float32)


def dot_nt(a, b):
    return lax.dot_general(a, b, (((1,), (1,)), ((), ())), preferred_element_type=jnp.float32)


def attend(layout, owner_slot, *refs):
    piece_count, near_count, after_count, chunk_head, by_slot, old_count, head = layout
    q_any, own_any, weight_any = refs[:3]
    pieces, refs = refs[3 : 3 + piece_count], refs[3 + piece_count :]
    near, refs = refs[:near_count], refs[near_count:]
    old, rest = refs[:old_count], refs[old_count + after_count :]
    dq_any, proj_any, own_any_grad = rest[:3]
    parts = rest[3 : 4 if by_slot else 5]
    (
        far_ref, own_ref, out_grad, weight, proj, att, s_ref, p_ref, qs, ups, q_t, up_t,
        m_ref, l_ref, acc_ref, own_grad, slots, far_sem, slot_sem, q_sem, piece_sem, sem,
    ) = rest[3 + len(parts) :]
    me = lax.axis_index("node")
    node_count = owner_slot.shape[0]
    tree_node = jnp.int32(0)
    for n in range(node_count):
        tree_node = jnp.where(owner_slot[n] == me, n, tree_node)
    tree_nodes = CHAIN + LEAVES
    first_node = tree_node // tree_nodes * tree_nodes
    depth = jnp.minimum(tree_node - first_node, CHAIN)
    lineage = [owner_slot[first_node + b] for b in range(CHAIN)]

    def ancestor(b):
        return lineage[b] if isinstance(b, int) else owner_slot[first_node + b]

    rows = qs.shape[0]
    heads = rows // NODE_LEN
    half = HEAD_DIM
    width = heads * HEAD_DIM
    factor = score_scale * log2_e
    stride = slots.shape[0] // 4

    def head_rows(h):
        return pl.ds(h * NODE_LEN, NODE_LEN)

    def head_columns(h, first=0):
        return pl.ds(first + h * HEAD_DIM, HEAD_DIM)

    q_copies = [
        pltpu.make_async_copy(
            q_any.at[:, head_columns(h, head * width)], qs.at[head_rows(h), :], q_sem.at[h]
        )
        for h in range(heads)
    ]
    def pair_copies(source, target, sems):
        return [
            pltpu.make_async_copy(
                source.at[:, pl.ds(i * source.shape[1] // 2 + chunk_head * half, half)],
                target.at[:, pl.ds(i * half, half)],
                sems[i],
            )
            for i in range(2)
        ]

    own_copies = pair_copies(own_any, own_ref, [sem.at[0], sem.at[2]])
    weight_copy = pltpu.make_async_copy(
        weight_any.at[pl.ds(head * width, width), :], weight, sem.at[1]
    )
    order = lax.axis_index("tp") if piece_count == 2 else 0
    piece_rows = pieces[0].shape[0]
    piece_copies = [
        pltpu.make_async_copy(
            piece,
            out_grad.at[pl.ds(pl.multiple_of((order ^ i) * piece_rows, piece_rows), piece_rows), :],
            piece_sem.at[i],
        )
        for i, piece in enumerate(pieces)
    ]
    for copy in own_copies + q_copies:
        copy.start()

    def far_copies(source, index, b):
        return pair_copies(
            source.at[index], far_ref.at[b], [far_sem.at[b], far_sem.at[CHAIN + b]]
        )

    def fetch(b, carry):
        if near_count == 1:
            for copy in far_copies(near[0], ancestor(b), b):
                copy.start()
            return carry
        away = ancestor(b) ^ me
        for kind in range(near_count):

            @pl.when(away % 4 == kind)
            def _():
                for copy in far_copies(near[kind], away // 4, b):
                    copy.start()

        return carry

    lax.fori_loop(0, depth, fetch, 0)

    late_copies = [weight_copy] + piece_copies
    if head > 0:
        late_copies.append(pltpu.make_async_copy(old[1], proj, sem.at[3]))
    for copy in late_copies:
        copy.start()

    def fold_max(s):
        return jnp.maximum(s[:, :half], s[:, half:])

    for copy in own_copies + q_copies:
        copy.wait()
    s = dot_nt(qs[...], own_ref[:, :half])
    row = lax.broadcasted_iota(jnp.int32, (rows, NODE_LEN), 0) % NODE_LEN
    col = lax.broadcasted_iota(jnp.int32, (rows, NODE_LEN), 1)
    s = jnp.where(col <= row, s, masked_score)
    s_ref[CHAIN] = s
    m_ref[...] = fold_max(s)

    def score_block(b, carry):
        for copy in far_copies(near[0], 0, b):
            copy.wait()
        s = dot_nt(qs[...], far_ref[b, :, :half])
        s_ref[b] = s
        m_ref[...] = jnp.maximum(m_ref[...], fold_max(s))
        return carry

    lax.fori_loop(0, depth, score_block, 0)
    m_ref[...] = jnp.broadcast_to(jnp.max(m_ref[...], axis=1, keepdims=True), (rows, half))

    def weigh(b, values):
        top = m_ref[...]
        s = s_ref[b]
        p_low = jnp.exp2((s[:, :half] - top) * factor)
        p_high = jnp.exp2((s[:, half:] - top) * factor)
        p = jnp.concatenate([p_low, p_high], axis=1).astype(jnp.bfloat16)
        p_ref[b] = p
        return p_low + p_high, dot(p, values)

    part_sum, part = weigh(CHAIN, own_ref[:, half:])
    l_ref[...] = part_sum
    acc_ref[...] = part

    def forward_block(b, carry):
        part_sum, part = weigh(b, far_ref[b, :, half:])
        l_ref[...] += part_sum
        acc_ref[...] += part
        return carry

    lax.fori_loop(0, depth, forward_block, 0)
    inverse = 1.0 / jnp.broadcast_to(jnp.sum(l_ref[...], axis=1, keepdims=True), (rows, half))
    l_ref[...] = inverse
    attended = (acc_ref[...] * inverse).astype(jnp.bfloat16)
    for h in range(heads):
        att[:, head_columns(h)] = attended[h * NODE_LEN : (h + 1) * NODE_LEN, :]

    for copy in late_copies:
        copy.wait()
    for h in range(0, heads, 2):
        count = min(2, heads - h)
        two = dot_nt(out_grad[...], weight[h * HEAD_DIM : (h + count) * HEAD_DIM, :])
        for i in range(count):
            ups[head_rows(h + i), :] = two[:, i * HEAD_DIM : (i + 1) * HEAD_DIM].astype(jnp.bfloat16)

    def project(n, carry):
        columns = pl.ds(pl.multiple_of(n * COLUMNS, COLUMNS), COLUMNS)
        share = dot(att[...], weight[:, columns])
        proj[:, columns] = share if head == 0 else proj[:, columns] + share
        return carry

    lax.fori_loop(0, weight.shape[1] // COLUMNS, project, 0)
    proj_out = pltpu.make_async_copy(proj, proj_any, sem.at[4])
    proj_out.start()

    upstream = ups[...].astype(jnp.float32)
    corr_ref = m_ref
    corr_ref[...] = jnp.broadcast_to(
        jnp.sum(upstream * attended.astype(jnp.float32), axis=1, keepdims=True), (rows, half)
    )
    q_t[...] = (qs[...].astype(jnp.float32) * (inverse * score_scale)).astype(jnp.bfloat16).T
    up_t[...] = (upstream * inverse).astype(jnp.bfloat16).T

    def backward(b, keys, values):
        corr = corr_ref[...]
        p = p_ref[b]
        d_prob = dot_nt(ups[...], values)
        centred = jnp.concatenate([d_prob[:, :half] - corr, d_prob[:, half:] - corr], axis=1)
        d_score = (p.astype(jnp.float32) * centred).astype(jnp.bfloat16)
        grad = jnp.concatenate([dot(q_t[...], d_score), dot(up_t[...], p)], axis=0)
        return dot(d_score, keys), grad

    def slot_place(b):
        if by_slot:
            return ancestor(b)
        away = ancestor(b) ^ me
        kind = away % 4
        return away // 4 + stride * jnp.where(kind == 0, 0, jnp.where(kind == 2, 1, 2 + kind // 2))

    slots[...] = jnp.zeros_like(slots)
    part, grad = backward(CHAIN, own_ref[:, :half], own_ref[:, half:])
    acc_ref[...] = part
    own_grad[...] = grad.T
    own_out = pltpu.make_async_copy(own_grad, own_any_grad, sem.at[3])
    own_out.start()

    def backward_block(b, carry):
        part, grad = backward(b, far_ref[b, :, :half], far_ref[b, :, half:])
        acc_ref[...] += part
        block = grad.astype(jnp.bfloat16).T
        slots[slot_place(b)] = block
        return carry

    lax.fori_loop(0, depth, backward_block, 0)
    if by_slot:
        part_copies = [pltpu.make_async_copy(slots, parts[0].at[:, head], slot_sem.at[0])]
    else:
        part_copies = [
            pltpu.make_async_copy(slots.at[pl.ds(2 * stride * i, 2 * stride)], part, slot_sem.at[i])
            for i, part in enumerate(parts)
        ]
    for copy in part_copies:
        copy.start()
    query_grad = (acc_ref[...] * (l_ref[...] * score_scale)).astype(jnp.bfloat16)
    for h in range(heads):
        att[:, head_columns(h)] = query_grad[h * NODE_LEN : (h + 1) * NODE_LEN, :]
    dq_out = pltpu.make_async_copy(att, dq_any.at[:, pl.ds(head * width, width)], sem.at[5])
    dq_out.start()
    for copy in part_copies + [own_out]:
        copy.wait()
    proj_out.wait()
    dq_out.wait()


def attention(
    head, chunk_head, head_group, nodes, slot_heads,
    owner_slot, query_rows, own, weight, pieces, near, old, after,
):
    bf16, f32 = jnp.bfloat16, jnp.float32
    stride = nodes // 4
    width = head_group * HEAD_DIM
    rows = head_group * NODE_LEN
    d_out = weight.shape[1]
    block = (NODE_LEN, PAIR)
    anywhere = pl.BlockSpec(memory_space=pl.ANY)
    in_smem = pl.BlockSpec(memory_space=pltpu.SMEM)
    if slot_heads:
        parts = [jax.ShapeDtypeStruct((nodes, slot_heads) + block, bf16)]
    else:
        parts = [jax.ShapeDtypeStruct((2 * stride,) + block, bf16)] * 2
    first_old = 4 + len(pieces) + len(near)
    aliases = {first_old + i: i if i < 2 else 3 for i in range(len(old))}
    layout = (len(pieces), len(near), len(after), chunk_head, bool(slot_heads), len(old), head)
    blocks = (CHAIN + 1) * head_group
    return pl.pallas_call(
        functools.partial(attend, layout),
        in_specs=[in_smem] + [anywhere] * (3 + len(pieces) + len(near) + len(old) + len(after)),
        out_specs=[anywhere] * (3 + len(parts)),
        out_shape=[
            jax.ShapeDtypeStruct(query_rows.shape, bf16),
            jax.ShapeDtypeStruct((NODE_LEN, d_out), f32),
            jax.ShapeDtypeStruct(block, f32),
        ]
        + parts,
        input_output_aliases=aliases,
        scratch_shapes=[
            pltpu.VMEM((CHAIN,) + block, bf16),
            pltpu.VMEM(block, bf16),
            pltpu.VMEM((NODE_LEN, d_out), bf16),
            pltpu.VMEM((width, d_out), bf16),
            pltpu.VMEM((NODE_LEN, d_out), f32),
            pltpu.VMEM((NODE_LEN, width), bf16),
            pltpu.VMEM((CHAIN + 1, rows, NODE_LEN), f32),
            pltpu.VMEM((CHAIN + 1, rows, NODE_LEN), bf16),
            pltpu.VMEM((rows, HEAD_DIM), bf16),
            pltpu.VMEM((rows, HEAD_DIM), bf16),
            pltpu.VMEM((HEAD_DIM, rows), bf16),
            pltpu.VMEM((HEAD_DIM, rows), bf16),
            pltpu.VMEM((rows, HEAD_DIM), f32),
            pltpu.VMEM((rows, HEAD_DIM), f32),
            pltpu.VMEM((rows, HEAD_DIM), f32),
            pltpu.VMEM(block, f32),
            pltpu.VMEM((nodes,) + block, bf16),
            pltpu.SemaphoreType.DMA((2 * CHAIN,)),
            pltpu.SemaphoreType.DMA((2,)),
            pltpu.SemaphoreType.DMA((head_group,)),
            pltpu.SemaphoreType.DMA((2,)),
            pltpu.SemaphoreType.DMA((6,)),
        ],
        compiler_params=pltpu.CompilerParams(vmem_limit_bytes=63 * 1024 * 1024),
        cost_estimate=pl.CostEstimate(
            flops=2 * blocks * NODE_LEN,
            bytes_accessed=2**20,
            transcendentals=0,
        ),
    )(owner_slot, query_rows, own, weight, *pieces, *near, *old, *after)


def zero_of(value):
    return jnp.minimum(jnp.abs(value.reshape(-1)[0].astype(jnp.float32)), 0.0)


def swap(block, mask, nodes):
    return lax.ppermute(block, "node", [(i, i ^ mask) for i in range(nodes)])


def gather_near(own, nodes, before):
    stride = nodes // 4
    line = jnp.stack([own] + [swap(own, 4 * d, nodes) for d in range(1, stride)])
    cross = swap(line, 2, nodes) + zero_of(before).astype(line.dtype)
    return [line, swap(line, 1, nodes), cross, swap(cross, 1, nodes)]


def add_level_1(keep, cross, came_keep, came_cross, cross_sum, keep_sum):
    f32 = jnp.float32
    cross_sum[...] = (cross[...].astype(f32) + came_cross[...].astype(f32)).astype(jnp.bfloat16)
    keep_sum[...] = keep[...].astype(f32) + came_keep[...].astype(f32)


def add_level_2(keep, came, keep_sum, *sent):
    total = keep[0] + came[0].astype(jnp.float32)
    for d in range(len(sent) + 1):

        @pl.when(pl.program_id(0) == d)
        def _():
            if d == 0:
                keep_sum[...] = total
            else:
                sent[d - 1][...] = total.astype(jnp.bfloat16)


def add_all(*refs):
    *parts, total = refs
    total[...] = functools.reduce(jnp.add, [part[...].astype(jnp.float32) for part in parts]).astype(total.dtype)


def small_call(kernel, grid, in_specs, out_specs, out_shape, operands, after):
    def run(*refs):
        kernel(*refs[: len(operands)], *refs[len(operands) + len(after) :])

    return pl.pallas_call(
        run,
        grid=grid,
        in_specs=in_specs + [pl.BlockSpec(memory_space=pl.ANY)] * len(after),
        out_specs=out_specs,
        out_shape=out_shape,
        compiler_params=pltpu.CompilerParams(vmem_limit_bytes=16 * 1024 * 1024),
        cost_estimate=pl.CostEstimate(flops=2**10, bytes_accessed=2**12, transcendentals=0),
    )(*operands, *after)


def scatter_sum(kept, away, own_part, nodes):
    bf16, f32 = jnp.bfloat16, jnp.float32
    stride = nodes // 4
    came = swap(away, 1, nodes)
    after = yield [away]
    block = kept.shape[1:]
    one = pl.BlockSpec((1,) + block, lambda d: (d, 0, 0))
    far = pl.BlockSpec((1,) + block, lambda d: (stride + d, 0, 0))
    whole = pl.BlockSpec(block, lambda d: (0, 0))
    cross, keep = small_call(
        add_level_1,
        (stride,),
        [one, far, one, far],
        [one, one],
        [jax.ShapeDtypeStruct((stride,) + block, t) for t in (bf16, f32)],
        [kept, kept, came, came],
        after,
    )
    came = swap(cross, 2, nodes)
    after = yield [cross]
    keep, *sent = small_call(
        add_level_2,
        (stride,),
        [one, one],
        [whole] * stride,
        [jax.ShapeDtypeStruct(block, f32)] + [jax.ShapeDtypeStruct(block, bf16)] * (stride - 1),
        [keep, came],
        after,
    )
    came = [swap(part, 4 * (d + 1), nodes) for d, part in enumerate(sent)]
    after = yield sent
    parts = [own_part, keep] + came
    return small_call(
        add_all, (1,), [whole] * len(parts), whole, jax.ShapeDtypeStruct(block, bf16), parts, after
    )


def local(tp, nodes, query_rows, key_rows, value_rows, out_weight, out_grad, owner_slot):
    bf16, f32 = jnp.bfloat16, jnp.float32
    kv_width = key_rows.shape[1]
    kv_heads = kv_width // HEAD_DIM
    head_group = query_rows.shape[1] // kv_width
    if tp == 2:
        pieces = [out_grad, lax.ppermute(out_grad, "tp", [(0, 1), (1, 0)])]
    else:
        pieces = [lax.all_gather(out_grad, "tp", axis=0, tiled=True)]

    own, near = {}, {}
    for first, heads in [(0, 1)] + ([(1, kv_heads - 1)] if kv_heads > 1 else []):
        columns = slice(first * HEAD_DIM, (first + heads) * HEAD_DIM)
        packed = jnp.concatenate([key_rows[:, columns], value_rows[:, columns]], axis=1)
        if first == 0:
            blocks = gather_near(packed, nodes, pieces[-1])
        else:
            blocks = [lax.all_gather(packed, "node", axis=0, tiled=False)]
        for i in range(heads):
            own[first + i], near[first + i] = (packed, i), blocks

    offloaded = max(0, kv_heads - 2)
    old, sums, own_parts, sent = [], [], [], []
    for k in range(kv_heads):
        by_slot = k < offloaded
        dq, proj, own_part, *parts = attention(
            k, own[k][1], head_group, nodes, offloaded if by_slot else 0,
            owner_slot, query_rows, own[k][0], out_weight, pieces, near[k], old, sent,
        )
        old = [dq, proj] + (parts if k + 1 < offloaded else [])
        sent = [own_part]
        if by_slot:
            own_parts.append(own_part)
            if k + 1 == offloaded:
                came = lax.psum_scatter(parts[0], "node", scatter_dimension=0, tiled=False)
        else:
            sums.append(scatter_sum(*parts, own_part, nodes))
            sent = next(sums[-1])
            if k + 1 < kv_heads:
                sent = sums[-1].send([])

    *earlier, last = sums
    early = [chain.send([own_part])[0] for chain in earlier] + [own_part]
    middle = last.send([early[0]])[0]
    rows = proj.shape[0] // tp
    if tp == 2:
        me = lax.axis_index("tp")
        away = lax.dynamic_slice_in_dim(proj, (1 - me) * rows, rows, 0)
        away = (away + zero_of(early[0])).astype(bf16)
        here = lax.dynamic_slice_in_dim(proj, me * rows, rows, 0)
        projected = here + lax.ppermute(away, "tp", [(0, 1), (1, 0)]).astype(f32)
        projected = projected.astype(bf16)
    else:
        projected = lax.psum_scatter(proj.astype(bf16), "tp", scatter_dimension=0, tiled=True)
    moved = last.send([middle])[0]
    totals = []
    for chain in earlier + [last]:
        try:
            chain.send([moved] if chain is last else [moved, projected])
        except StopIteration as end:
            totals.append(end.value)
    if offloaded:
        totals = [(own_parts[k] + came[k].astype(f32)).astype(bf16) for k in range(offloaded)] + totals
    return (
        projected,
        dq,
        jnp.concatenate([total[:, :HEAD_DIM] for total in totals], axis=1),
        jnp.concatenate([total[:, HEAD_DIM:] for total in totals], axis=1),
    )


def solution(mesh):
    in_specs = (
        P("node", "tp"),
        P("node", "tp"),
        P("node", "tp"),
        P("tp", None),
        P(("node", "tp"), None),
        P(),
    )
    out_specs = (P(("node", "tp"), None), P("node", "tp"), P("node", "tp"), P("node", "tp"))
    return jax.shard_map(
        functools.partial(local, mesh.shape["tp"], mesh.shape["node"]),
        mesh=mesh, in_specs=in_specs, out_specs=out_specs, check_vma=False,
    )
```

```python
import functools

import jax
import jax.numpy as jnp
from jax import lax
from jax.experimental import pallas as pl
from jax.experimental.pallas import tpu as pltpu
from jax.sharding import PartitionSpec as P

HEAD_DIM = 128
NODE_LEN = 256
CHAIN = 8
LEAVES = 8
PAIR = 2 * HEAD_DIM
COLUMNS = 512

masked_score = -1e30
score_scale = HEAD_DIM ** (-0.5)
log2_e = 1.4426950408889634


def dot(a, b):
    return jnp.dot(a, b, preferred_element_type=jnp.float32)


def dot_nt(a, b):
    return lax.dot_general(a, b, (((1,), (1,)), ((), ())), preferred_element_type=jnp.float32)


def attend(layout, owner_slot, *refs):
    piece_count, near_count, after_count, chunk_head, by_slot, old_count, head = layout
    q_any, own_any, weight_any = refs[:3]
    pieces, refs = refs[3 : 3 + piece_count], refs[3 + piece_count :]
    near, refs = refs[:near_count], refs[near_count:]
    old, rest = refs[:old_count], refs[old_count + after_count :]
    dq_any, proj_any, own_any_grad = rest[:3]
    parts = rest[3 : 4 if by_slot else 5]
    (
        far_ref, own_ref, out_grad, weight, proj, att, s_ref, p_ref, qs, ups, q_t, up_t,
        m_ref, l_ref, acc_ref, own_grad, slots, far_sem, slot_sem, q_sem, piece_sem, sem,
    ) = rest[3 + len(parts) :]
    me = lax.axis_index("node")
    node_count = owner_slot.shape[0]
    tree_node = jnp.int32(0)
    for n in range(node_count):
        tree_node = jnp.where(owner_slot[n] == me, n, tree_node)
    tree_nodes = CHAIN + LEAVES
    first_node = tree_node // tree_nodes * tree_nodes
    depth = jnp.minimum(tree_node - first_node, CHAIN)
    lineage = [owner_slot[first_node + b] for b in range(CHAIN)]

    def ancestor(b):
        return lineage[b] if isinstance(b, int) else owner_slot[first_node + b]

    rows = qs.shape[0]
    heads = rows // NODE_LEN
    half = HEAD_DIM
    width = heads * HEAD_DIM
    factor = score_scale * log2_e
    stride = slots.shape[0] // 4

    def head_rows(h):
        return pl.ds(h * NODE_LEN, NODE_LEN)

    def head_columns(h, first=0):
        return pl.ds(first + h * HEAD_DIM, HEAD_DIM)

    q_copies = [
        pltpu.make_async_copy(
            q_any.at[:, head_columns(h, head * width)], qs.at[head_rows(h), :], q_sem.at[h]
        )
        for h in range(heads)
    ]
    def pair_copies(source, target, sems):
        return [
            pltpu.make_async_copy(
                source.at[:, pl.ds(i * source.shape[1] // 2 + chunk_head * half, half)],
                target.at[:, pl.ds(i * half, half)],
                sems[i],
            )
            for i in range(2)
        ]

    own_copies = pair_copies(own_any, own_ref, [sem.at[0], sem.at[2]])
    weight_copy = pltpu.make_async_copy(
        weight_any.at[pl.ds(head * width, width), :], weight, sem.at[1]
    )
    order = lax.axis_index("tp") if piece_count == 2 else 0
    piece_rows = pieces[0].shape[0]
    piece_copies = [
        pltpu.make_async_copy(
            piece,
            out_grad.at[pl.ds(pl.multiple_of((order ^ i) * piece_rows, piece_rows), piece_rows), :],
            piece_sem.at[i],
        )
        for i, piece in enumerate(pieces)
    ]
    for copy in own_copies + q_copies:
        copy.start()

    def far_copies(source, index, b):
        return pair_copies(
            source.at[index], far_ref.at[b], [far_sem.at[b], far_sem.at[CHAIN + b]]
        )

    def fetch(b, carry):
        if near_count == 1:
            for copy in far_copies(near[0], ancestor(b), b):
                copy.start()
            return carry
        away = ancestor(b) ^ me
        for kind in range(near_count):

            @pl.when(away % 4 == kind)
            def _():
                for copy in far_copies(near[kind], away // 4, b):
                    copy.start()

        return carry

    lax.fori_loop(0, depth, fetch, 0)

    late_copies = [weight_copy] + piece_copies
    if head > 0:
        late_copies.append(pltpu.make_async_copy(old[1], proj, sem.at[3]))
    for copy in late_copies:
        copy.start()

    def fold_max(s):
        return jnp.maximum(s[:, :half], s[:, half:])

    for copy in own_copies + q_copies:
        copy.wait()
    s = dot_nt(qs[...], own_ref[:, :half])
    row = lax.broadcasted_iota(jnp.int32, (rows, NODE_LEN), 0) % NODE_LEN
    col = lax.broadcasted_iota(jnp.int32, (rows, NODE_LEN), 1)
    s = jnp.where(col <= row, s, masked_score)
    s_ref[CHAIN] = s
    m_ref[...] = fold_max(s)

    def score_block(b, carry):
        for copy in far_copies(near[0], 0, b):
            copy.wait()
        s = dot_nt(qs[...], far_ref[b, :, :half])
        s_ref[b] = s
        m_ref[...] = jnp.maximum(m_ref[...], fold_max(s))
        return carry

    lax.fori_loop(0, depth, score_block, 0)
    m_ref[...] = jnp.broadcast_to(jnp.max(m_ref[...], axis=1, keepdims=True), (rows, half))

    def weigh(b, values):
        top = m_ref[...]
        s = s_ref[b]
        p_low = jnp.exp2((s[:, :half] - top) * factor)
        p_high = jnp.exp2((s[:, half:] - top) * factor)
        p = jnp.concatenate([p_low, p_high], axis=1).astype(jnp.bfloat16)
        p_ref[b] = p
        return p_low + p_high, dot(p, values)

    part_sum, part = weigh(CHAIN, own_ref[:, half:])
    l_ref[...] = part_sum
    acc_ref[...] = part

    def forward_block(b, carry):
        part_sum, part = weigh(b, far_ref[b, :, half:])
        l_ref[...] += part_sum
        acc_ref[...] += part
        return carry

    lax.fori_loop(0, depth, forward_block, 0)
    inverse = 1.0 / jnp.broadcast_to(jnp.sum(l_ref[...], axis=1, keepdims=True), (rows, half))
    l_ref[...] = inverse
    attended = (acc_ref[...] * inverse).astype(jnp.bfloat16)
    for h in range(heads):
        att[:, head_columns(h)] = attended[h * NODE_LEN : (h + 1) * NODE_LEN, :]

    for copy in late_copies:
        copy.wait()
    for h in range(0, heads, 2):
        count = min(2, heads - h)
        two = dot_nt(out_grad[...], weight[h * HEAD_DIM : (h + count) * HEAD_DIM, :])
        for i in range(count):
            ups[head_rows(h + i), :] = two[:, i * HEAD_DIM : (i + 1) * HEAD_DIM].astype(jnp.bfloat16)

    def project(n, carry):
        columns = pl.ds(pl.multiple_of(n * COLUMNS, COLUMNS), COLUMNS)
        share = dot(att[...], weight[:, columns])
        proj[:, columns] = share if head == 0 else proj[:, columns] + share
        return carry

    lax.fori_loop(0, weight.shape[1] // COLUMNS, project, 0)
    proj_out = pltpu.make_async_copy(proj, proj_any, sem.at[4])
    proj_out.start()

    upstream = ups[...].astype(jnp.float32)
    corr_ref = m_ref
    corr_ref[...] = jnp.broadcast_to(
        jnp.sum(upstream * attended.astype(jnp.float32), axis=1, keepdims=True), (rows, half)
    )
    q_t[...] = (qs[...].astype(jnp.float32) * (inverse * score_scale)).astype(jnp.bfloat16).T
    up_t[...] = (upstream * inverse).astype(jnp.bfloat16).T

    def backward(b, keys, values):
        corr = corr_ref[...]
        p = p_ref[b]
        d_prob = dot_nt(ups[...], values)
        centred = jnp.concatenate([d_prob[:, :half] - corr, d_prob[:, half:] - corr], axis=1)
        d_score = (p.astype(jnp.float32) * centred).astype(jnp.bfloat16)
        grad = jnp.concatenate([dot(q_t[...], d_score), dot(up_t[...], p)], axis=0)
        return dot(d_score, keys), grad

    def slot_place(b):
        if by_slot:
            return ancestor(b)
        away = ancestor(b) ^ me
        kind = away % 4
        return away // 4 + stride * jnp.where(kind == 0, 0, jnp.where(kind == 2, 1, 2 + kind // 2))

    slots[...] = jnp.zeros_like(slots)
    part, grad = backward(CHAIN, own_ref[:, :half], own_ref[:, half:])
    acc_ref[...] = part
    own_grad[...] = grad.T
    own_out = pltpu.make_async_copy(own_grad, own_any_grad, sem.at[3])
    own_out.start()

    def backward_block(b, carry):
        part, grad = backward(b, far_ref[b, :, :half], far_ref[b, :, half:])
        acc_ref[...] += part
        block = grad.astype(jnp.bfloat16).T
        slots[slot_place(b)] = block
        return carry

    lax.fori_loop(0, depth, backward_block, 0)
    if by_slot:
        part_copies = [pltpu.make_async_copy(slots, parts[0].at[:, head], slot_sem.at[0])]
    else:
        part_copies = [
            pltpu.make_async_copy(slots.at[pl.ds(2 * stride * i, 2 * stride)], part, slot_sem.at[i])
            for i, part in enumerate(parts)
        ]
    for copy in part_copies:
        copy.start()
    query_grad = (acc_ref[...] * (l_ref[...] * score_scale)).astype(jnp.bfloat16)
    for h in range(heads):
        att[:, head_columns(h)] = query_grad[h * NODE_LEN : (h + 1) * NODE_LEN, :]
    dq_out = pltpu.make_async_copy(att, dq_any.at[:, pl.ds(head * width, width)], sem.at[5])
    dq_out.start()
    for copy in part_copies + [own_out]:
        copy.wait()
    proj_out.wait()
    dq_out.wait()


def attention(
    head, chunk_head, head_group, nodes, slot_heads,
    owner_slot, query_rows, own, weight, pieces, near, old, after,
):
    bf16, f32 = jnp.bfloat16, jnp.float32
    stride = nodes // 4
    width = head_group * HEAD_DIM
    rows = head_group * NODE_LEN
    d_out = weight.shape[1]
    block = (NODE_LEN, PAIR)
    anywhere = pl.BlockSpec(memory_space=pl.ANY)
    in_smem = pl.BlockSpec(memory_space=pltpu.SMEM)
    if slot_heads:
        parts = [jax.ShapeDtypeStruct((nodes, slot_heads) + block, bf16)]
    else:
        parts = [jax.ShapeDtypeStruct((2 * stride,) + block, bf16)] * 2
    first_old = 4 + len(pieces) + len(near)
    aliases = {first_old + i: i if i < 2 else 3 for i in range(len(old))}
    layout = (len(pieces), len(near), len(after), chunk_head, bool(slot_heads), len(old), head)
    blocks = (CHAIN + 1) * head_group
    return pl.pallas_call(
        functools.partial(attend, layout),
        in_specs=[in_smem] + [anywhere] * (3 + len(pieces) + len(near) + len(old) + len(after)),
        out_specs=[anywhere] * (3 + len(parts)),
        out_shape=[
            jax.ShapeDtypeStruct(query_rows.shape, bf16),
            jax.ShapeDtypeStruct((NODE_LEN, d_out), f32),
            jax.ShapeDtypeStruct(block, f32),
        ]
        + parts,
        input_output_aliases=aliases,
        scratch_shapes=[
            pltpu.VMEM((CHAIN,) + block, bf16),
            pltpu.VMEM(block, bf16),
            pltpu.VMEM((NODE_LEN, d_out), bf16),
            pltpu.VMEM((width, d_out), bf16),
            pltpu.VMEM((NODE_LEN, d_out), f32),
            pltpu.VMEM((NODE_LEN, width), bf16),
            pltpu.VMEM((CHAIN + 1, rows, NODE_LEN), f32),
            pltpu.VMEM((CHAIN + 1, rows, NODE_LEN), bf16),
            pltpu.VMEM((rows, HEAD_DIM), bf16),
            pltpu.VMEM((rows, HEAD_DIM), bf16),
            pltpu.VMEM((HEAD_DIM, rows), bf16),
            pltpu.VMEM((HEAD_DIM, rows), bf16),
            pltpu.VMEM((rows, HEAD_DIM), f32),
            pltpu.VMEM((rows, HEAD_DIM), f32),
            pltpu.VMEM((rows, HEAD_DIM), f32),
            pltpu.VMEM(block, f32),
            pltpu.VMEM((nodes,) + block, bf16),
            pltpu.SemaphoreType.DMA((2 * CHAIN,)),
            pltpu.SemaphoreType.DMA((2,)),
            pltpu.SemaphoreType.DMA((head_group,)),
            pltpu.SemaphoreType.DMA((2,)),
            pltpu.SemaphoreType.DMA((6,)),
        ],
        compiler_params=pltpu.CompilerParams(vmem_limit_bytes=63 * 1024 * 1024),
        cost_estimate=pl.CostEstimate(
            flops=2 * blocks * NODE_LEN,
            bytes_accessed=2**20,
            transcendentals=0,
        ),
    )(owner_slot, query_rows, own, weight, *pieces, *near, *old, *after)


def zero_of(value):
    return jnp.minimum(jnp.abs(value.reshape(-1)[0].astype(jnp.float32)), 0.0)


def swap(block, mask, nodes):
    return lax.ppermute(block, "node", [(i, i ^ mask) for i in range(nodes)])


def gather_near(own, nodes, before):
    stride = nodes // 4
    line = jnp.stack([own] + [swap(own, 4 * d, nodes) for d in range(1, stride)])
    cross = swap(line, 2, nodes) + zero_of(before).astype(line.dtype)
    return [line, swap(line, 1, nodes), cross, swap(cross, 1, nodes)]


def add_level_1(keep, cross, came_keep, came_cross, cross_sum, keep_sum):
    f32 = jnp.float32
    cross_sum[...] = (cross[...].astype(f32) + came_cross[...].astype(f32)).astype(jnp.bfloat16)
    keep_sum[...] = keep[...].astype(f32) + came_keep[...].astype(f32)


def add_level_2(keep, came, keep_sum, *sent):
    total = keep[0] + came[0].astype(jnp.float32)
    for d in range(len(sent) + 1):

        @pl.when(pl.program_id(0) == d)
        def _():
            if d == 0:
                keep_sum[...] = total
            else:
                sent[d - 1][...] = total.astype(jnp.bfloat16)


def add_all(*refs):
    *parts, total = refs
    total[...] = functools.reduce(jnp.add, [part[...].astype(jnp.float32) for part in parts]).astype(total.dtype)


def small_call(kernel, grid, in_specs, out_specs, out_shape, operands, after):
    def run(*refs):
        kernel(*refs[: len(operands)], *refs[len(operands) + len(after) :])

    return pl.pallas_call(
        run,
        grid=grid,
        in_specs=in_specs + [pl.BlockSpec(memory_space=pl.ANY)] * len(after),
        out_specs=out_specs,
        out_shape=out_shape,
        compiler_params=pltpu.CompilerParams(vmem_limit_bytes=16 * 1024 * 1024),
        cost_estimate=pl.CostEstimate(flops=2**10, bytes_accessed=2**12, transcendentals=0),
    )(*operands, *after)


def scatter_sum(kept, away, own_part, nodes):
    bf16, f32 = jnp.bfloat16, jnp.float32
    stride = nodes // 4
    came = swap(away, 1, nodes)
    after = yield [away]
    block = kept.shape[1:]
    one = pl.BlockSpec((1,) + block, lambda d: (d, 0, 0))
    far = pl.BlockSpec((1,) + block, lambda d: (stride + d, 0, 0))
    whole = pl.BlockSpec(block, lambda d: (0, 0))
    cross, keep = small_call(
        add_level_1,
        (stride,),
        [one, far, one, far],
        [one, one],
        [jax.ShapeDtypeStruct((stride,) + block, t) for t in (bf16, f32)],
        [kept, kept, came, came],
        after,
    )
    came = swap(cross, 2, nodes)
    after = yield [cross]
    keep, *sent = small_call(
        add_level_2,
        (stride,),
        [one, one],
        [whole] * stride,
        [jax.ShapeDtypeStruct(block, f32)] + [jax.ShapeDtypeStruct(block, bf16)] * (stride - 1),
        [keep, came],
        after,
    )
    came = [swap(part, 4 * (d + 1), nodes) for d, part in enumerate(sent)]
    after = yield sent
    parts = [own_part, keep] + came
    return small_call(
        add_all, (1,), [whole] * len(parts), whole, jax.ShapeDtypeStruct(block, bf16), parts, after
    )


def local(tp, nodes, query_rows, key_rows, value_rows, out_weight, out_grad, owner_slot):
    bf16, f32 = jnp.bfloat16, jnp.float32
    kv_width = key_rows.shape[1]
    kv_heads = kv_width // HEAD_DIM
    head_group = query_rows.shape[1] // kv_width
    if tp == 2:
        pieces = [out_grad, lax.ppermute(out_grad, "tp", [(0, 1), (1, 0)])]
    else:
        pieces = [lax.all_gather(out_grad, "tp", axis=0, tiled=True)]

    own, near = {}, {}
    for first, heads in [(0, 1)] + ([(1, kv_heads - 1)] if kv_heads > 1 else []):
        columns = slice(first * HEAD_DIM, (first + heads) * HEAD_DIM)
        packed = jnp.concatenate([key_rows[:, columns], value_rows[:, columns]], axis=1)
        if first == 0:
            blocks = gather_near(packed, nodes, pieces[-1])
        else:
            blocks = [lax.all_gather(packed, "node", axis=0, tiled=False)]
        for i in range(heads):
            own[first + i], near[first + i] = (packed, i), blocks

    offloaded = max(0, kv_heads - 2)
    old, sums, own_parts, sent = [], [], [], []
    for k in range(kv_heads):
        by_slot = k < offloaded
        dq, proj, own_part, *parts = attention(
            k, own[k][1], head_group, nodes, offloaded if by_slot else 0,
            owner_slot, query_rows, own[k][0], out_weight, pieces, near[k], old, sent,
        )
        old = [dq, proj] + (parts if k + 1 < offloaded else [])
        sent = [own_part]
        if by_slot:
            own_parts.append(own_part)
            if k + 1 == offloaded:
                came = lax.psum_scatter(parts[0], "node", scatter_dimension=0, tiled=False)
        else:
            sums.append(scatter_sum(*parts, own_part, nodes))
            sent = next(sums[-1])
            if k + 1 < kv_heads:
                sent = sums[-1].send([])

    *earlier, last = sums
    early = [chain.send([own_part])[0] for chain in earlier] + [own_part]
    middle = last.send([early[0]])[0]
    rows = proj.shape[0] // tp
    if tp == 2:
        me = lax.axis_index("tp")
        away = lax.dynamic_slice_in_dim(proj, (1 - me) * rows, rows, 0)
        away = (away + zero_of(early[0])).astype(bf16)
        here = lax.dynamic_slice_in_dim(proj, me * rows, rows, 0)
        projected = here + lax.ppermute(away, "tp", [(0, 1), (1, 0)]).astype(f32)
        projected = projected.astype(bf16)
    else:
        projected = lax.psum_scatter(proj.astype(bf16), "tp", scatter_dimension=0, tiled=True)
    moved = last.send([middle])[0]
    totals = []
    for chain in earlier + [last]:
        try:
            chain.send([moved])
        except StopIteration as end:
            totals.append(end.value)
    if offloaded:
        totals = [(own_parts[k] + came[k].astype(f32)).astype(bf16) for k in range(offloaded)] + totals
    return (
        projected,
        dq,
        jnp.concatenate([total[:, :HEAD_DIM] for total in totals], axis=1),
        jnp.concatenate([total[:, HEAD_DIM:] for total in totals], axis=1),
    )


def solution(mesh):
    in_specs = (
        P("node", "tp"),
        P("node", "tp"),
        P("node", "tp"),
        P("tp", None),
        P(("node", "tp"), None),
        P(),
    )
    out_specs = (P(("node", "tp"), None), P("node", "tp"), P("node", "tp"), P("node", "tp"))
    return jax.shard_map(
        functools.partial(local, mesh.shape["tp"], mesh.shape["node"]),
        mesh=mesh, in_specs=in_specs, out_specs=out_specs, check_vma=False,
    )
```
